128 devices in a mesh: dp: 4 (over x_hi, core), seq: 32 (over z, y, x_lo).
Axes of the slice: x: 4 (x_hi: 2, x_lo: 2; x = x_hi * 2 + x_lo), y: 4, z: 4, core: 2. Of those that a mesh axis runs over, the one named last changes fastest.
Arguments:
- latent: bfloat16 [4, 16384, 3072], P('dp', 'seq'), may hold values from -6 to 6
- mod_scale: float32 [4, 3072], P('dp'), may hold values from 0.5 to 2
- mod_shift: float32 [4, 3072], P('dp'), may hold values from -4 to 4
- w_query: bfloat16 [3072, 1536], P(('dp', 'seq')), may hold values from -0.109375 to 0.109375
- w_key: bfloat16 [3072, 1536], P(('dp', 'seq')), may hold values from -0.109375 to 0.109375
- w_value: bfloat16 [3072, 1536], P(('dp', 'seq')), may hold values from -0.109375 to 0.109375
- cache_keys: bfloat16 [4, 16384, 1536], P('dp', 'seq'), may hold values from -96 to 96
- cache_values: bfloat16 [4, 16384, 1536], P('dp', 'seq'), may hold values from -6 to 6
- block_lists: int32 [4, 32, 4], P('dp', 'seq'), may hold values from -1 to 31, as said below
Outputs:
- context: bfloat16 [4, 16384, 1536], P('dp', 'seq')
The draws below stay inside these ranges and needn't reach their ends.
Inputs may be any that keep to these rules, and one draw needn't show every extreme that they name: `block_lists`: each row lists distinct blocks b' of the same clip with |b' - b| <= 2 for its own block b, live entries first, then -1.
All inputs are finite; a program needn't handle non-finite values.
Results may differ from the reference program's by a relative error of at most 0.0065.
The reference program's roundings to bfloat16 on the way (of `normed`, `query` and `probs`) count: a program that leaves them out, or rounds other values in their place, can miss the bound.
Values may be sent and summed in bfloat16 or wider, within the bound.
No kernel may reach another device: no remote copies, remote signals or barrier semaphores. Data moves between devices by JAX's collectives and lax.ppermute only.
A program may use at most 192 MiB of HBM per device.

```python
import math
import jax
import jax.numpy as jnp
from jax import lax

D = 3072
HEADS = 12
HS = 128
BLK = 512
WIN = 2
LMAX = 4
HD = 1536
CLIPS = 4
NBLK = 32
FRAMES = 16384


def draw_block_lists(key, part):
    key = jax.random.fold_in(key, 5)
    first_key, second_key = jax.random.split(key)
    span = 2 * WIN + 1
    blocks = jnp.arange(NBLK, dtype=jnp.int32)[None, :, None]
    offsets = jnp.arange(span, dtype=jnp.int32)[None, None, :] - WIN
    candidates = jnp.broadcast_to(blocks + offsets, (CLIPS, NBLK, span))
    valid = (candidates >= 0) & (candidates < NBLK)
    noise = jax.random.randint(first_key, (CLIPS, NBLK, span), 0, 1024, dtype=jnp.int32)
    score = jnp.where(valid, 16384, 0) + noise * 8 + jnp.arange(span, dtype=jnp.int32)
    order = jnp.argsort(-score, axis=-1)
    chosen = jnp.take_along_axis(candidates, order, axis=-1)[..., :LMAX]
    count = jnp.sum(valid.astype(jnp.int32), axis=-1)
    length = jax.random.randint(second_key, (CLIPS, NBLK), 0, LMAX + 1, dtype=jnp.int32)
    length = length.at[:, NBLK // 2].set(LMAX)
    length = length.at[:, NBLK - 1].set(LMAX)
    length = jnp.minimum(length, count)
    slots = jnp.arange(LMAX, dtype=jnp.int32)
    return jnp.where(slots[None, None, :] < length[..., None], chosen, -1).astype(jnp.int32)


def draw_cache_keys(key, part):
    key = jax.random.fold_in(key, 11)
    first_key = jax.random.fold_in(key, 0)
    noise = jnp.clip(jax.random.normal(first_key, (CLIPS, FRAMES, HEADS * HS), dtype=jnp.float32), -6.0, 6.0)
    result = noise
    return result.astype(jnp.bfloat16)


def block_levels(key, shape, shards, smallest, top_value):
    def one(axis_at, shards_of):
        draws = jax.random.uniform(jax.random.fold_in(jax.random.fold_in(key, 6), axis_at), (shards_of,), jnp.float32, smallest / len(shards), top_value / len(shards))
        return jnp.repeat(jnp.exp(draws), shape[axis_at] // shards_of).reshape((-1,) + (1,) * (len(shape) - axis_at - 1))

    loudness = one(*shards[0])
    for cut in shards[1:]:
        loudness = loudness * one(*cut)
    return loudness


def centred(stream_key, dims, width, bound, cuts=(), held_as=jnp.bfloat16):
    gain = block_levels(stream_key, dims, cuts, -0.22, 0.18) if cuts else 1.0
    values = jax.random.normal(stream_key, dims, jnp.float32) * width * gain
    return jnp.minimum(jnp.maximum(values, -bound), bound).astype(held_as)


def setup_inputs(seed: int = 0) -> dict:
    arg_keys = jax.random.split(jax.random.key(seed), 10)
    latent = centred(arg_keys[0], (CLIPS, FRAMES, D), 1.0, 6.0, ((0, 4), (1, 32)))
    mod_scale = jnp.clip(0.5 + 1.5 * jax.random.uniform(arg_keys[1], (CLIPS, D), jnp.float32) ** block_levels(arg_keys[1], (CLIPS, D), ((0, 4),), -0.2, 0.2), 0.5, 2.0)
    mod_shift = centred(arg_keys[2], (CLIPS, D), 1.0, 4.0, ((0, 4),), jnp.float32)
    w_query = centred(arg_keys[3], (D, HD), D ** -0.5, 0.109375, ((0, 128),))
    w_key = centred(arg_keys[4], (D, HD), D ** -0.5, 0.109375, ((0, 128),))
    w_value = centred(arg_keys[5], (D, HD), D ** -0.5, 0.109375, ((0, 128),))
    cache_keys = draw_cache_keys(jax.random.fold_in(arg_keys[9], 71), 0)
    cache_values = centred(arg_keys[7], (CLIPS, FRAMES, HD), 1.0, 6.0, ((0, 4), (1, 32)))
    block_lists = draw_block_lists(jax.random.fold_in(arg_keys[9], 71), 0)
    return dict(latent=latent, mod_scale=mod_scale, mod_shift=mod_shift, w_query=w_query, w_key=w_key, w_value=w_value, cache_keys=cache_keys, cache_values=cache_values, block_lists=block_lists)


def reference(latent, mod_scale, mod_shift, w_query, w_key, w_value, cache_keys, cache_values, block_lists):
    wide = HEADS * HS
    values_in = latent.astype(jnp.float32)
    factor = lax.rsqrt(lax.optimization_barrier(jnp.mean(values_in * values_in, axis=-1, keepdims=True)) + 1e-06)
    normed = (values_in * factor * mod_scale[:, None, :] + mod_shift[:, None, :]).astype(jnp.bfloat16)
    flat = normed.reshape(CLIPS * FRAMES, D)
    query = jnp.dot(flat, w_query, preferred_element_type=jnp.float32).astype(jnp.bfloat16).reshape(CLIPS, FRAMES, wide)
    keys_now = jnp.dot(flat, w_key, preferred_element_type=jnp.float32).astype(jnp.bfloat16).reshape(CLIPS, FRAMES, wide)
    values_now = jnp.dot(flat, w_value, preferred_element_type=jnp.float32).astype(jnp.bfloat16).reshape(CLIPS, FRAMES, wide)
    margin = WIN * BLK
    padded_keys = jnp.pad(cache_keys, ((0, 0), (margin, margin), (0, 0)))
    padded_values = jnp.pad(cache_values, ((0, 0), (margin, margin), (0, 0)))
    span = 2 * WIN + 1

    def one_block(index):
        clip = (index // NBLK).astype(jnp.int32)
        block = (index % NBLK).astype(jnp.int32)
        start = (block * BLK).astype(jnp.int32)
        zero = jnp.int32(0)
        query_block = lax.dynamic_slice(query, (clip, start, zero), (1, BLK, wide))[0]
        fresh_keys = lax.dynamic_slice(keys_now, (clip, start, zero), (1, BLK, wide))[0]
        fresh_values = lax.dynamic_slice(values_now, (clip, start, zero), (1, BLK, wide))[0]
        near_keys = lax.dynamic_slice(padded_keys, (clip, start, zero), (1, span * BLK, wide))[0]
        near_values = lax.dynamic_slice(padded_values, (clip, start, zero), (1, span * BLK, wide))[0]
        listed = lax.dynamic_slice(block_lists, (clip, block, zero), (1, 1, LMAX))[0, 0]
        targets = block + jnp.arange(-WIN, WIN + 1, dtype=jnp.int32)
        flags = jnp.any(listed[None, :] == targets[:, None], axis=1)
        valid = jnp.concatenate([jnp.ones((1,), dtype=bool), flags])
        columns = jnp.repeat(valid, BLK)
        key_set = jnp.concatenate([fresh_keys, near_keys], axis=0).astype(jnp.float32).reshape(-1, HEADS, HS)
        value_set = jnp.concatenate([fresh_values, near_values], axis=0).astype(jnp.float32).reshape(-1, HEADS, HS)
        query_heads = query_block.astype(jnp.float32).reshape(BLK, HEADS, HS)
        scores = jnp.einsum('qhd,khd->hqk', query_heads, key_set) / math.sqrt(HS)
        scores = jnp.where(columns[None, None, :], scores, -jnp.inf)
        largest = lax.optimization_barrier(jnp.max(scores, axis=-1, keepdims=True))
        weights = jnp.exp(scores - largest)
        total = lax.optimization_barrier(jnp.sum(weights, axis=-1))
        probs = lax.optimization_barrier(weights.astype(jnp.bfloat16)).astype(jnp.float32)
        summed = jnp.einsum('hqk,khd->qhd', probs, value_set)
        result = summed / jnp.transpose(total)[:, :, None]
        return result.reshape(BLK, wide).astype(jnp.bfloat16)
    blocks_out = lax.map(one_block, jnp.arange(CLIPS * NBLK, dtype=jnp.int32))
    return blocks_out.reshape(CLIPS, FRAMES, wide)
```

```python
import functools
import itertools
import math

import jax
import jax.numpy as jnp
from jax import lax
from jax.experimental import pallas as pl
from jax.experimental.pallas import tpu as pltpu
from jax.sharding import Mesh
from jax.sharding import PartitionSpec as P

HEADS = 12
HS = 128
NX, NZ, NY = 2, 4, 4
AXES = ("xh", "c", "z", "y", "xl")
DIMS = (2, 2, 4, 4, 2)
BF = jnp.bfloat16
F32 = jnp.float32
HALF = HEADS // 2


def flat(place):
    index = 0
    for at, size in zip(place, DIMS):
        index = index * size + at
    return index


def permuted(value, move):
    places = itertools.product(*(range(n) for n in DIMS))
    moves = ((place, move(*place)) for place in places)
    return lax.ppermute(value, AXES, [(flat(p), flat(q)) for p, q in moves if q is not None])


def other_core(xh, c, z, y, xl):
    return xh, 1 - c, z, y, xl


def along_z(step):
    return lambda xh, c, z, y, xl: (xh, c, (z + step) % NZ, y, xl)


def along_x(xh, c, z, y, xl):
    return xh, c, z, y, 1 - xl


def along_blocks(step):
    def move(xh, c, z, y, xl):
        at = z * NY + y + step
        return (xh, c, at // NY, at % NY, xl) if 0 <= at < NZ * NY else None

    return move


def diagonal(xh, c, z, y, xl):
    return along_blocks(1 if xl == 0 else -1)(xh, c, z, y, xl)


def project_kernel(z_ref, mine_ref, other_ref, w0, wb, wa, wt, wu, mine_out, other_out):
    z = z_ref[0]
    depth = wt.shape[0]
    for src, dst in ((mine_ref, mine_out), (other_ref, other_out)):
        acc = jnp.dot(src[z], w0[...], preferred_element_type=F32)
        acc += jnp.dot(src[(z + 3) % 4], wb[...], preferred_element_type=F32)
        acc += jnp.dot(src[(z + 1) % 4], wa[...], preferred_element_type=F32)
        far = src.at[(z + 2) % 4]
        acc += jnp.dot(far[:, :depth], wt[...], preferred_element_type=F32)
        acc += jnp.dot(far[:, depth:], wu[...], preferred_element_type=F32)
        dst[...] = acc.astype(BF)


def project(z, mine, other, pieces):
    rows, depth = mine.shape[1:]
    wide = pieces[0].shape[1]
    tile = 256
    whole = [pl.BlockSpec(p.shape, lambda i, z_ref: (0, 0)) for p in pieces]
    source = pl.BlockSpec((4, tile, depth), lambda i, z_ref: (0, i, 0))
    target = pl.BlockSpec((tile, wide), lambda i, z_ref: (i, 0))
    return pl.pallas_call(
        project_kernel,
        grid_spec=pltpu.PrefetchScalarGridSpec(
            num_scalar_prefetch=1,
            grid=(rows // tile,),
            in_specs=[source, source, *whole],
            out_specs=[target, target],
        ),
        out_shape=[jax.ShapeDtypeStruct((rows, wide), BF)] * 2,
        compiler_params=pltpu.CompilerParams(vmem_limit_bytes=48 << 20),
        cost_estimate=pl.CostEstimate(
            flops=2 * 2 * rows * 4 * depth * wide,
            bytes_accessed=2 * 2 * rows * (4 * depth + wide) + 8 * depth * wide,
            transcendentals=0,
        ),
    )(z, mine, other, *pieces)


def attend_kernel(flags, *refs):
    queries, keys, values = refs[0:2], refs[2:4], refs[4:6]
    cached_keys, cached_values = refs[6:16], refs[16:26]
    outs = refs[26:28]
    tops, sums, accs = refs[28:31]
    factor = math.log2(math.e) / math.sqrt(HS)

    def scores(half, key):
        return (
            lax.dot_general(
                queries[half][...], key[...], (((1,), (1,)), ((), ())), preferred_element_type=F32
            )
            * factor
        )

    for half in range(2):
        s = scores(half, keys[half])
        top = jnp.max(s, axis=-1, keepdims=True)
        p = jnp.exp2(s - top)
        tops[half] = jnp.broadcast_to(top, tops.shape[1:])
        sums[half] = jnp.broadcast_to(jnp.sum(p, axis=-1, keepdims=True), sums.shape[1:])
        accs[half] = jnp.dot(p.astype(BF), values[half][...], preferred_element_type=F32)
    for n in range(5):

        @pl.when(flags[n] > 0)
        def _():
            for half in range(2):
                s = scores(half, cached_keys[2 * n + half])
                old = tops[half][:, :1]
                top = jnp.maximum(old, jnp.max(s, axis=-1, keepdims=True))
                p = jnp.exp2(s - top)
                scale = jnp.exp2(old - top)
                tops[half] = jnp.broadcast_to(top, tops.shape[1:])
                total = sums[half][:, :1] * scale + jnp.sum(p, axis=-1, keepdims=True)
                sums[half] = jnp.broadcast_to(total, sums.shape[1:])
                accs[half] = accs[half] * scale + jnp.dot(
                    p.astype(BF), cached_values[2 * n + half][...], preferred_element_type=F32
                )

    for half in range(2):
        outs[half][...] = (accs[half] / sums[half][:, :1]).astype(BF)


def attend(flags, queries, keys, values, cached_keys, cached_values):
    rows = queries[0].shape[0]
    near = pl.BlockSpec((rows, HS), lambda g, flags: (0, g))
    halves = [
        pl.BlockSpec((rows, HS), lambda g, flags: (0, flags[5] * HALF + g)),
        pl.BlockSpec((rows, HS), lambda g, flags: (0, (1 - flags[5]) * HALF + g)),
    ]
    twice = lambda arrays: [a for a in arrays for _ in range(2)]
    out = jax.ShapeDtypeStruct((rows, HALF * HS), BF)
    return pl.pallas_call(
        attend_kernel,
        grid_spec=pltpu.PrefetchScalarGridSpec(
            num_scalar_prefetch=1,
            grid=(HALF,),
            in_specs=[near] * 6 + halves * 10,
            out_specs=[near, near],
            scratch_shapes=[
                pltpu.VMEM((2, rows, HS), F32),
                pltpu.VMEM((2, rows, HS), F32),
                pltpu.VMEM((2, rows, HS), F32),
            ],
        ),
        out_shape=[out, out],
        compiler_params=pltpu.CompilerParams(vmem_limit_bytes=48 << 20),
        cost_estimate=pl.CostEstimate(
            flops=6 * 4 * rows * rows * HEADS * HS,
            bytes_accessed=14 * 2 * rows * HEADS * HS,
            transcendentals=6 * rows * rows * HEADS,
        ),
    )(flags, *queries, *keys, *values, *twice(cached_keys), *twice(cached_values))


def body(
    latent, mod_scale, mod_shift, w_query, w_key, w_value, cache_keys, cache_values, block_lists
):
    core = lax.axis_index("c")
    z, y, xl = lax.axis_index("z"), lax.axis_index("y"), lax.axis_index("xl")
    own_keys, own_values = cache_keys[0], cache_values[0]
    rows = latent.shape[1]

    stacked = jnp.concatenate([w_query, w_key, w_value], axis=0)
    left, right = stacked[:, : HALF * HS], stacked[:, HALF * HS :]
    first = core == 0
    kept, sent = jnp.where(first, left, right), jnp.where(first, right, left)
    got = permuted(sent, other_core)
    thin = w_query.shape[0]
    shape = (3, 1, thin, HALF * HS)
    kept, got = kept.reshape(shape), got.reshape(shape)
    pair = jnp.concatenate([jnp.where(first, kept, got), jnp.where(first, got, kept)], axis=1)
    ring = lax.all_gather(pair.reshape(3, 2 * thin, HALF * HS), ("xh", "xl"), axis=0, tiled=False)
    plane = lax.all_gather(ring, "y", axis=0, tiled=False)
    plane = jnp.moveaxis(plane.reshape(16, 3, 2 * thin, HALF * HS), 1, 0)
    plane = plane.reshape(3, 16 * 2 * thin, HALF * HS)

    values_in = latent[0].astype(F32)
    factor = lax.rsqrt(jnp.mean(values_in * values_in, axis=-1, keepdims=True) + 1e-06)
    normed = (values_in * factor * mod_scale[0][None, :] + mod_shift[0][None, :]).astype(BF)
    depth = 16 * 2 * thin
    by_z = jnp.transpose(normed.reshape(rows, 4, 4, depth // 4), (2, 0, 1, 3)).reshape(4, rows, depth)
    place = lax.broadcasted_iota(jnp.int32, (depth, depth), 1)
    row = place % thin
    at_c = place // thin % 2
    at_xl = place // (2 * thin) % 2
    at_xh = place // (4 * thin) % 2
    at_y = place // (8 * thin)
    wanted = (((at_xh * 2 + at_c) * 4 + at_y) * 2 + at_xl) * thin + row
    order = (lax.broadcasted_iota(jnp.int32, (depth, depth), 0) == wanted).astype(BF)
    mine = lax.dot_general(by_z, order, (((2,), (0,)), ((), ())), preferred_element_type=BF)
    other = permuted(mine, other_core)

    x_keys, x_values = permuted(own_keys, along_x), permuted(own_values, along_x)
    before_values = permuted(own_values, along_blocks(1))
    after_values = permuted(own_values, along_blocks(-1))
    before_keys = permuted(own_keys, along_blocks(1))
    after_keys = permuted(own_keys, along_blocks(-1))
    far_values = permuted(jnp.where(xl == 1, before_values, after_values), along_x)
    far_keys = permuted(x_keys, diagonal)

    block = (z * NY + y) * 2 + xl
    listed = block_lists[0, 0]
    side = jnp.where(xl == 0, 1, -1)
    offsets = (0 * side, side, 0 * side - 2, 0 * side + 2, -side)
    flags = [jnp.any(listed == block + offset).astype(jnp.int32) for offset in offsets]
    flags = jnp.stack([*flags, core.astype(jnp.int32)])

    z_index = z.astype(jnp.int32)[None]
    results = []
    for n in range(3):
        piece = plane[n]
        below = permuted(piece, along_z(1))
        above = permuted(piece, along_z(-1))
        top = permuted(below[: depth // 2], along_z(1))
        bottom = permuted(above[depth // 2 :], along_z(-1))
        own, theirs = project(z_index, mine, other, (piece, below, above, top, bottom))
        results.append((own, permuted(theirs, other_core)))

    context = attend(
        flags,
        *results,
        (own_keys, x_keys, before_keys, after_keys, far_keys),
        (own_values, x_values, before_values, after_values, far_values),
    )
    low = jnp.where(first, context[0], context[1])
    high = jnp.where(first, context[1], context[0])
    return jnp.concatenate([low, high], axis=1)[None]


def solution(mesh):
    fine = Mesh(mesh.devices.reshape(DIMS), AXES)
    dp, seq = ("xh", "c"), ("z", "y", "xl")
    placed = (
        P(dp, seq, None),
        P(dp, None),
        P(dp, None),
        P(dp + seq, None),
        P(dp + seq, None),
        P(dp + seq, None),
        P(dp, seq, None),
        P(dp, seq, None),
        P(dp, seq, None),
    )
    return jax.shard_map(
        body, mesh=fine, in_specs=placed, out_specs=P(dp, seq, None), check_vma=False
    )
```

```python
import itertools
import math

import jax
import jax.numpy as jnp
from jax import lax
from jax.experimental import pallas as pl
from jax.experimental.pallas import tpu as pltpu
from jax.sharding import Mesh
from jax.sharding import PartitionSpec as P

HS = 128
NZ, NY = 4, 4
AXES = ("xh", "c", "z", "y", "xl")
DIMS = (2, 2, 4, 4, 2)
BF = jnp.bfloat16
F32 = jnp.float32


def flat(place):
    index = 0
    for at, size in zip(place, DIMS):
        index = index * size + at
    return index


def permuted(value, move):
    places = itertools.product(*(range(n) for n in DIMS))
    moves = ((place, move(*place)) for place in places)
    return lax.ppermute(value, AXES, [(flat(p), flat(q)) for p, q in moves if q is not None])


def other_core(xh, c, z, y, xl):
    return xh, 1 - c, z, y, xl


def other_half(xh, c, z, y, xl):
    return 1 - xh, c, z, y, xl


def partner(xh, c, z, y, xl):
    return xh, c, z, y, 1 - xl


def along_z(step):
    return lambda xh, c, z, y, xl: (xh, c, (z + step) % NZ, y, xl)


def along_y(step):
    return lambda xh, c, z, y, xl: (xh, c, z, (y + step) % NY, xl)


def along_pairs(step):
    def move(xh, c, z, y, xl):
        at = z * NY + y + step
        return (xh, c, at // NY, at % NY, xl) if 0 <= at < NZ * NY else None

    return move


def after(value, *earlier):
    return lax.optimization_barrier((value, *earlier))[0]


def project_kernel(where_ref, src_ref, *refs):
    mine, theirs, out, held = refs[0:5], refs[5:10], refs[10], refs[11]
    z, core = where_ref[0], where_ref[1]
    tensors, deep = mine[0].shape[:2]
    short = deep // 2

    @pl.when(pl.program_id(0) == 0)
    def _():
        for pieces, at in ((mine, core), (theirs, 1 - core)):
            start = pl.multiple_of(at * deep, 64)
            own, below, above, top, bottom = pieces
            for t in range(tensors):
                held[t, z, pl.ds(start, deep)] = own[t]
                held[t, (z + 3) % 4, pl.ds(start, deep)] = below[t]
                held[t, (z + 1) % 4, pl.ds(start, deep)] = above[t]
                held[t, (z + 2) % 4, pl.ds(start, short)] = top[t]
                held[t, (z + 2) % 4, pl.ds(pl.multiple_of(start + short, 64), short)] = bottom[t]

    for t in range(tensors):
        acc = jnp.dot(src_ref[0], held[t, 0], preferred_element_type=F32)
        for n in range(1, 4):
            acc += jnp.dot(src_ref[n], held[t, n], preferred_element_type=F32)
        out[t] = acc.astype(BF)


def project(where, source, mine, theirs):
    rows, depth = source.shape[1:]
    tensors, _, wide = mine[0].shape
    tile = 256
    pieces = [*mine, *theirs]
    return pl.pallas_call(
        project_kernel,
        grid_spec=pltpu.PrefetchScalarGridSpec(
            num_scalar_prefetch=1,
            grid=(rows // tile,),
            in_specs=[
                pl.BlockSpec((4, tile, depth), lambda i, where: (0, i, 0)),
                *[pl.BlockSpec(p.shape, lambda i, where: (0, 0, 0)) for p in pieces],
            ],
            out_specs=pl.BlockSpec((tensors, tile, wide), lambda i, where: (0, i, 0)),
            scratch_shapes=[pltpu.VMEM((tensors, 4, depth, wide), BF)],
        ),
        out_shape=jax.ShapeDtypeStruct((tensors, rows, wide), BF),
        compiler_params=pltpu.CompilerParams(vmem_limit_bytes=50 << 20),
        cost_estimate=pl.CostEstimate(
            flops=2 * rows * 4 * depth * wide * tensors,
            bytes_accessed=2 * rows * (4 * depth + wide * tensors) + 8 * depth * wide * tensors,
            transcendentals=0,
        ),
    )(where, source, *pieces)


STEP = 3


def attend_kernel(flags, query_ref, *refs):
    sources, out = refs[:14], refs[14]
    tops, sums, accs = refs[15:18]
    factor = math.log2(math.e) / math.sqrt(HS)
    cuts = [slice(h * HS, (h + 1) * HS) for h in range(STEP)]

    def scores(key_ref, h):
        return lax.dot_general(
            key_ref[0, :, cuts[h]],
            query_ref[0, :, cuts[h]],
            (((1,), (1,)), ((), ())),
            preferred_element_type=F32,
        )

    def absorb(key_ref, value_ref, first):
        ahead = scores(key_ref, 0)
        for h in range(STEP):
            s = ahead
            if h + 1 < STEP:
                ahead = scores(key_ref, h + 1)
            top = jnp.max(s, axis=0, keepdims=True)
            if not first:
                old = tops[h, :1]
                top = jnp.maximum(old, top)
            p = jnp.exp2((s - top) * factor)
            total = jnp.sum(p, axis=0, keepdims=True)
            summed = lax.dot_general(
                value_ref[0, :, cuts[h]],
                p.astype(BF),
                (((0,), (0,)), ((), ())),
                preferred_element_type=F32,
            )
            if not first:
                scale = jnp.exp2((old - top) * factor)
                total += sums[h, :1] * scale
                summed += accs[h] * scale
            tops[h, :1] = top
            sums[h, :1] = total
            accs[h] = summed

    absorb(sources[0], sources[1], True)
    for n in range(6):

        @pl.when(flags[n] > 0)
        def _():
            absorb(sources[2 * n + 2], sources[2 * n + 3], False)

    for h in range(STEP):
        out[:, cuts[h]] = (accs[h] / sums[h, :1]).T.astype(BF)


def attend(flags, query, sources):
    _, rows, wide = query.shape
    heads = wide // HS
    at = lambda n: pl.BlockSpec((1, rows, STEP * HS), lambda g, flags: (n, 0, g))
    return pl.pallas_call(
        attend_kernel,
        grid_spec=pltpu.PrefetchScalarGridSpec(
            num_scalar_prefetch=1,
            grid=(heads // STEP,),
            in_specs=[at(0)] + [at(0), at(1)] * 7,
            out_specs=pl.BlockSpec((rows, STEP * HS), lambda g, flags: (0, g)),
            scratch_shapes=[
                pltpu.VMEM((STEP, 8, rows), F32),
                pltpu.VMEM((STEP, 8, rows), F32),
                pltpu.VMEM((STEP, HS, rows), F32),
            ],
        ),
        out_shape=jax.ShapeDtypeStruct((rows, wide), BF),
        compiler_params=pltpu.CompilerParams(vmem_limit_bytes=48 << 20),
        cost_estimate=pl.CostEstimate(
            flops=8 * 4 * rows * rows * wide,
            bytes_accessed=16 * 2 * rows * wide,
            transcendentals=4 * rows * rows * heads,
        ),
    )(flags, query, *[s for source in sources for s in (source, source)])


def body(
    latent, mod_scale, mod_shift, w_query, w_key, w_value, cache_keys, cache_values, block_lists
):
    core, xh = lax.axis_index("c"), lax.axis_index("xh")
    z, y, xl = lax.axis_index("z"), lax.axis_index("y"), lax.axis_index("xl")
    rows = latent.shape[1]
    thin, full = w_query.shape
    wide = full // 2
    even = xl == 0

    def halves(array):
        left, right = array[..., :wide], array[..., wide:]
        return jnp.where(even, left, right), jnp.where(even, right, left)

    def in_order(is_first, mine, theirs, axis):
        return jnp.concatenate(
            [jnp.where(is_first, mine, theirs), jnp.where(is_first, theirs, mine)], axis=axis
        )

    kept, sent = halves(jnp.stack([w_query, w_key, w_value]))
    pair = in_order(even, kept, permuted(sent, partner), 1)
    ring = in_order(xh == 0, pair, permuted(pair, other_half), 1)
    plane = jnp.zeros((3, NY, 4 * thin, wide), BF)
    for step in range(NY):
        piece = permuted(ring, along_y(-step)) if step else ring
        plane = lax.dynamic_update_slice(plane, piece[:, None], (0, (y + step) % NY, 0, 0))
    deep = NY * 4 * thin
    plane = plane.reshape(3, deep, wide)

    kv_mine, kv_sent = halves(jnp.stack([cache_keys[0], cache_values[0]]))
    listed = block_lists[0]
    kv_got = permuted(kv_sent, partner)
    lists = jnp.concatenate([listed, permuted(listed, partner)], axis=0)
    before_mine, after_mine = (permuted(kv_mine, along_pairs(step)) for step in (1, -1))
    before_got, after_got = (permuted(kv_got, along_pairs(step)) for step in (1, -1))
    cached = (kv_mine, kv_got, before_mine, before_got, after_mine, after_got)
    block = (z * NY + y) * 2 + xl
    other = block + jnp.where(even, 1, -1)
    named = jnp.stack([block, other, block - 2, other - 2, block + 2, other + 2])
    flags = jnp.any(lists[:, None, :] == named[None, :, None], axis=-1).astype(jnp.int32)

    values_in = latent[0].astype(F32)
    factor = lax.rsqrt(jnp.mean(values_in * values_in, axis=-1, keepdims=True) + 1e-06)
    normed = (values_in * factor * mod_scale[0][None, :] + mod_shift[0][None, :]).astype(BF)
    depth = 2 * deep
    by_z = jnp.transpose(normed.reshape(rows, 4, 4, depth // 4), (2, 0, 1, 3)).reshape(4, rows, depth)
    place = lax.broadcasted_iota(jnp.int32, (depth, depth), 1)
    row = place % thin
    at_xl = place // thin % 2
    at_xh = place // (2 * thin) % 2
    at_y = place // (4 * thin) % 4
    at_c = place // deep
    wanted = (((at_xh * 2 + at_c) * 4 + at_y) * 2 + at_xl) * thin + row
    order = (lax.broadcasted_iota(jnp.int32, (depth, depth), 0) == wanted).astype(BF)
    mine = lax.dot_general(by_z, order, (((2,), (0,)), ((), ())), preferred_element_type=BF)
    theirs = permuted(after(mine, kv_got), partner)

    where = jnp.stack([z, core]).astype(jnp.int32)
    across = permuted(plane, other_core)
    groups = []
    previous = ()
    for part in (slice(0, 1), slice(1, 3)):
        own = plane[part]
        below = permuted(after(own, *previous), along_z(1))
        above = permuted(after(own, *previous), along_z(-1))
        top = permuted(below[:, : deep // 2], along_z(1))
        bottom = permuted(above[:, deep // 2 :], along_z(-1))
        previous = (below, above)
        gathered = (below, above, top, bottom)
        swapped = [permuted(g, other_core) for g in gathered]
        groups.append(((own, *gathered), (across[part], *swapped)))

    results = []
    for n, source in ((1, theirs), (0, mine)):
        query = project(where, source, *groups[0])
        fresh = project(where, source, *groups[1])
        results.append(attend(flags[n], query, (fresh, *cached)))
    back = permuted(results[0], partner)
    return in_order(even, results[1], back, 1)[None]


def solution(mesh):
    fine = Mesh(mesh.devices.reshape(DIMS), AXES)
    dp, seq = ("xh", "c"), ("z", "y", "xl")
    placed = (
        P(dp, seq, None),
        P(dp, None),
        P(dp, None),
        P(dp + seq, None),
        P(dp + seq, None),
        P(dp + seq, None),
        P(dp, seq, None),
        P(dp, seq, None),
        P(dp, seq, None),
    )
    return jax.shard_map(
        body, mesh=fine, in_specs=placed, out_specs=P(dp, seq, None), check_vma=False
    )
```

```python
import functools
import itertools
import math

import jax
import jax.numpy as jnp
from jax import lax
from jax.experimental import pallas as pl
from jax.experimental.pallas import tpu as pltpu
from jax.sharding import Mesh
from jax.sharding import PartitionSpec as P

HS = 128
NZ, NY = 4, 4
AXES = ("xh", "c", "z", "y", "xl")
DIMS = (2, 2, 4, 4, 2)
BF = jnp.bfloat16
F32 = jnp.float32


def flat(place):
    index = 0
    for at, size in zip(place, DIMS):
        index = index * size + at
    return index


def permuted(value, move):
    places = itertools.product(*(range(n) for n in DIMS))
    moves = ((place, move(*place)) for place in places)
    return lax.ppermute(value, AXES, [(flat(p), flat(q)) for p, q in moves if q is not None])


def other_core(xh, c, z, y, xl):
    return xh, 1 - c, z, y, xl


def other_half(xh, c, z, y, xl):
    return 1 - xh, c, z, y, xl


def partner(xh, c, z, y, xl):
    return xh, c, z, y, 1 - xl


def along_z(step):
    return lambda xh, c, z, y, xl: (xh, c, (z + step) % NZ, y, xl)


def along_y(step):
    return lambda xh, c, z, y, xl: (xh, c, z, (y + step) % NY, xl)


def along_pairs(step):
    def move(xh, c, z, y, xl):
        at = z * NY + y + step
        return (xh, c, at // NY, at % NY, xl) if 0 <= at < NZ * NY else None

    return move


def after(value, *earlier):
    return lax.optimization_barrier((value, *earlier))[0]


def project_kernel(where_ref, src_ref, *refs):
    mine, theirs, out, held = refs[0:5], refs[5:10], refs[10], refs[11]
    z, core = where_ref[0], where_ref[1]
    tensors, deep = mine[0].shape[:2]
    short = deep // 2

    @pl.when(pl.program_id(0) == 0)
    def _():
        for pieces, at in ((mine, core), (theirs, 1 - core)):
            start = pl.multiple_of(at * deep, 64)
            own, below, above, top, bottom = pieces
            for t in range(tensors):
                held[t, z, pl.ds(start, deep)] = own[t]
                held[t, (z + 3) % 4, pl.ds(start, deep)] = below[t]
                held[t, (z + 1) % 4, pl.ds(start, deep)] = above[t]
                held[t, (z + 2) % 4, pl.ds(start, short)] = top[t]
                held[t, (z + 2) % 4, pl.ds(pl.multiple_of(start + short, 64), short)] = bottom[t]

    for t in range(tensors):
        acc = jnp.dot(src_ref[0], held[t, 0], preferred_element_type=F32)
        for n in range(1, 4):
            acc += jnp.dot(src_ref[n], held[t, n], preferred_element_type=F32)
        out[t] = acc.astype(BF)


def project(where, source, mine, theirs):
    rows, depth = source.shape[1:]
    tensors, _, wide = mine[0].shape
    tile = 256
    pieces = [*mine, *theirs]
    return pl.pallas_call(
        project_kernel,
        grid_spec=pltpu.PrefetchScalarGridSpec(
            num_scalar_prefetch=1,
            grid=(rows // tile,),
            in_specs=[
                pl.BlockSpec((4, tile, depth), lambda i, where: (0, i, 0)),
                *[pl.BlockSpec(p.shape, lambda i, where: (0, 0, 0)) for p in pieces],
            ],
            out_specs=pl.BlockSpec((tensors, tile, wide), lambda i, where: (0, i, 0)),
            scratch_shapes=[pltpu.VMEM((tensors, 4, depth, wide), BF)],
        ),
        out_shape=jax.ShapeDtypeStruct((tensors, rows, wide), BF),
        compiler_params=pltpu.CompilerParams(vmem_limit_bytes=50 << 20),
        cost_estimate=pl.CostEstimate(
            flops=2 * rows * 4 * depth * wide * tensors,
            bytes_accessed=2 * rows * (4 * depth + wide * tensors) + 8 * depth * wide * tensors,
            transcendentals=0,
        ),
    )(where, source, *pieces)


STEP = 3


def attend_kernel(flags, query_ref, *refs, fresh, cached, begun, ended):
    refs = list(refs)
    fresh_refs = [refs.pop(0) for _ in range(2 * fresh)]
    cached_refs = [refs.pop(0) for _ in range(2 * cached)]
    state_in = [refs.pop(0) for _ in range(3 * begun)]
    out = refs.pop(0) if ended else None
    state = refs
    factor = math.log2(math.e) / math.sqrt(HS)
    cuts = [slice(h * HS, (h + 1) * HS) for h in range(STEP)]

    def scores(key_ref, h):
        return lax.dot_general(
            key_ref[0, :, cuts[h]],
            query_ref[0, :, cuts[h]],
            (((1,), (1,)), ((), ())),
            preferred_element_type=F32,
        )

    def absorb(key_ref, value_ref, held, kept):
        ahead = scores(key_ref, 0)
        for h in range(STEP):
            s = ahead
            if h + 1 < STEP:
                ahead = scores(key_ref, h + 1)
            top = jnp.max(s, axis=0, keepdims=True)
            if held:
                old = held[0][h, :1]
                top = jnp.maximum(old, top)
            p = jnp.exp2((s - top) * factor)
            total = jnp.sum(p, axis=0, keepdims=True)
            summed = lax.dot_general(
                value_ref[0, :, cuts[h]],
                p.astype(BF),
                (((0,), (0,)), ((), ())),
                preferred_element_type=F32,
            )
            if held:
                scale = jnp.exp2((old - top) * factor)
                total += held[1][h, :1] * scale
                summed += held[2][h] * scale
            if kept:
                kept[0][h, :1] = top
                kept[1][h, :1] = total
                kept[2][h] = summed
            else:
                out[:, cuts[h]] = (summed / total).T.astype(BF)

    if fresh:
        last = ended and not cached
        absorb(*fresh_refs, state_in if begun else None, None if last else state)
    else:
        state[0][...] = jnp.full(state[0].shape, -jnp.inf, F32)
        state[1][...] = jnp.zeros(state[1].shape, F32)
        state[2][...] = jnp.zeros(state[2].shape, F32)
    for n in range(cached):

        @pl.when(flags[n] > 0)
        def _():
            absorb(cached_refs[2 * n], cached_refs[2 * n + 1], state, state)

    if ended and cached:
        for h in range(STEP):
            out[:, cuts[h]] = (state[2][h] / state[1][h, :1]).T.astype(BF)


def attend(flags, query, fresh, cached, groups, state=None, ended=True):
    rows = query.shape[1]
    first, count = groups
    at = lambda n: pl.BlockSpec((1, rows, STEP * HS), lambda g, flags: (n, 0, first + g))
    tall = [(STEP, 8, rows), (STEP, 8, rows), (STEP, HS, rows)]
    state_specs = [pl.BlockSpec(t, lambda g, flags: (g, 0, 0)) for t in tall]
    sources = [s for s in (*fresh, *cached) for _ in range(2)]
    blocks = 2 if not cached else 5
    kernel = functools.partial(
        attend_kernel,
        fresh=len(fresh),
        cached=len(cached),
        begun=state is not None,
        ended=ended,
    )
    heads = count * STEP
    return pl.pallas_call(
        kernel,
        grid_spec=pltpu.PrefetchScalarGridSpec(
            num_scalar_prefetch=1,
            grid=(count,),
            in_specs=[at(0)] + [at(0), at(1)] * (len(sources) // 2) + state_specs * (state is not None),
            out_specs=pl.BlockSpec((rows, STEP * HS), lambda g, flags: (0, g)) if ended else state_specs,
            scratch_shapes=[pltpu.VMEM(t, F32) for t in tall] if ended and cached else [],
        ),
        out_shape=jax.ShapeDtypeStruct((rows, heads * HS), BF)
        if ended
        else [jax.ShapeDtypeStruct((heads, *t[1:]), F32) for t in tall],
        compiler_params=pltpu.CompilerParams(vmem_limit_bytes=48 << 20),
        cost_estimate=pl.CostEstimate(
            flops=blocks * 8 * rows * rows * heads * HS,
            bytes_accessed=blocks * 4 * rows * heads * HS,
            transcendentals=blocks * rows * rows * heads,
        ),
    )(flags, query, *sources, *(state or ()))


def body(
    latent, mod_scale, mod_shift, w_query, w_key, w_value, cache_keys, cache_values, block_lists
):
    core, xh = lax.axis_index("c"), lax.axis_index("xh")
    z, y, xl = lax.axis_index("z"), lax.axis_index("y"), lax.axis_index("xl")
    rows = latent.shape[1]
    thin, full = w_query.shape
    wide = full // 2
    even = xl == 0

    def halves(array):
        left, right = array[..., :wide], array[..., wide:]
        return jnp.where(even, left, right), jnp.where(even, right, left)

    def in_order(is_first, mine, theirs, axis):
        return jnp.concatenate(
            [jnp.where(is_first, mine, theirs), jnp.where(is_first, theirs, mine)], axis=axis
        )

    listed = block_lists[0]
    lists = jnp.concatenate([listed, permuted(listed, partner)], axis=0)
    kv_mine, kv_sent = halves(jnp.stack([cache_keys[0], cache_values[0]]))
    near = [[permuted(kv_mine[:1], along_pairs(step))] for step in (1, -1)]

    kept, sent = halves(jnp.stack([w_query, w_key, w_value]))
    pair = in_order(even, kept, permuted(sent, partner), 1)
    ring = in_order(xh == 0, pair, permuted(pair, other_half), 1)
    kv_got = permuted(after(kv_sent, ring, lists), partner)
    ring = after(ring, near[0][0], near[1][0])
    plane = jnp.zeros((3, NY, 4 * thin, wide), BF)
    for step in range(NY):
        piece = permuted(ring, along_y(-step)) if step else ring
        plane = lax.dynamic_update_slice(plane, piece[:, None], (0, (y + step) % NY, 0, 0))
    deep = NY * 4 * thin
    plane = plane.reshape(3, deep, wide)
    late = after(kv_mine[1:], plane)
    for side, step in zip(near, (1, -1)):
        side.append(permuted(late, along_pairs(step)))

    values_in = latent[0].astype(F32)
    factor = lax.rsqrt(jnp.mean(values_in * values_in, axis=-1, keepdims=True) + 1e-06)
    normed = (values_in * factor * mod_scale[0][None, :] + mod_shift[0][None, :]).astype(BF)
    depth = 2 * deep
    by_z = jnp.transpose(normed.reshape(rows, 4, 4, depth // 4), (2, 0, 1, 3)).reshape(4, rows, depth)
    place = lax.broadcasted_iota(jnp.int32, (depth, depth), 1)
    row = place % thin
    at_xl = place // thin % 2
    at_xh = place // (2 * thin) % 2
    at_y = place // (4 * thin) % 4
    at_c = place // deep
    wanted = (((at_xh * 2 + at_c) * 4 + at_y) * 2 + at_xl) * thin + row
    order = (lax.broadcasted_iota(jnp.int32, (depth, depth), 0) == wanted).astype(BF)
    mine = lax.dot_general(by_z, order, (((2,), (0,)), ((), ())), preferred_element_type=BF)
    theirs = permuted(after(mine, kv_got), partner)

    where = jnp.stack([z, core]).astype(jnp.int32)
    half = deep // 2

    def z_ring(own):
        below, above = permuted(own, along_z(1)), permuted(own, along_z(-1))
        top = permuted(below[:, :half], along_z(1))
        bottom = permuted(above[:, half:], along_z(-1))
        return own, below, above, top, bottom

    swapped = lambda pieces: [permuted(p, other_core) for p in pieces]
    query_weights = z_ring(plane[:1])
    across = permuted(after(plane, near[0][1], near[1][1]), other_core)
    query_theirs = [across[:1], *swapped(after(p, near[0][1], near[1][1]) for p in query_weights[1:])]
    fresh_weights = z_ring(after(plane[1:], *query_weights[3:]))
    fresh_theirs = [across[1:], *swapped(fresh_weights[1:])]

    late = after(kv_got, across, *query_theirs)
    far = [permuted(late, along_pairs(step)) for step in (1, -1)]

    block = (z * NY + y) * 2 + xl
    other = block + jnp.where(even, 1, -1)
    named = jnp.stack([block, other, block - 2, block + 2, other - 2, other + 2])
    flags = jnp.any(lists[:, None, :] == named[None, :, None], axis=-1).astype(jnp.int32)
    pairs = [jnp.concatenate(side, axis=0) for side in near]
    cached = (kv_mine, kv_got, *pairs, *far)

    query = project(where, mine, query_weights, query_theirs)
    state = attend(flags[0], query, (), cached, (0, 2), ended=False)
    their_query = project(where, theirs, query_weights, query_theirs)
    their_fresh = project(where, theirs, fresh_weights, fresh_theirs)
    low = attend(flags[1], their_query, (their_fresh,), cached, (0, 1))
    low_back = permuted(low, partner)
    high = attend(flags[1], their_query, (their_fresh,), cached, (1, 1))
    high_back = permuted(high, partner)
    fresh = project(where, after(mine, high), fresh_weights, fresh_theirs)
    own = attend(flags[0], query, (fresh,), (), (0, 2), state)
    back = jnp.concatenate([low_back, high_back], axis=1)
    return in_order(even, own, back, 1)[None]


def solution(mesh):
    fine = Mesh(mesh.devices.reshape(DIMS), AXES)
    dp, seq = ("xh", "c"), ("z", "y", "xl")
    placed = (
        P(dp, seq, None),
        P(dp, None),
        P(dp, None),
        P(dp + seq, None),
        P(dp + seq, None),
        P(dp + seq, None),
        P(dp, seq, None),
        P(dp, seq, None),
        P(dp, seq, None),
    )
    return jax.shard_map(
        body, mesh=fine, in_specs=placed, out_specs=P(dp, seq, None), check_vma=False
    )
```

```python
import functools
import itertools
import math

import jax
import jax.numpy as jnp
from jax import lax
from jax.experimental import pallas as pl
from jax.experimental.pallas import tpu as pltpu
from jax.sharding import Mesh
from jax.sharding import PartitionSpec as P

HS = 128
NZ, NY = 4, 4
AXES = ("xh", "c", "z", "y", "xl")
DIMS = (2, 2, 4, 4, 2)
BF = jnp.bfloat16
F32 = jnp.float32


def flat(place):
    index = 0
    for at, size in zip(place, DIMS):
        index = index * size + at
    return index


def permuted(value, move):
    places = itertools.product(*(range(n) for n in DIMS))
    moves = ((place, move(*place)) for place in places)
    return lax.ppermute(value, AXES, [(flat(p), flat(q)) for p, q in moves if q is not None])


def other_core(xh, c, z, y, xl):
    return xh, 1 - c, z, y, xl


def other_half(xh, c, z, y, xl):
    return 1 - xh, c, z, y, xl


def partner(xh, c, z, y, xl):
    return xh, c, z, y, 1 - xl


def along_z(step):
    return lambda xh, c, z, y, xl: (xh, c, (z + step) % NZ, y, xl)


def along_y(step):
    return lambda xh, c, z, y, xl: (xh, c, z, (y + step) % NY, xl)


def along_pairs(step):
    def move(xh, c, z, y, xl):
        at = z * NY + y + step
        return (xh, c, at // NY, at % NY, xl) if 0 <= at < NZ * NY else None

    return move


def after(value, *earlier):
    return lax.optimization_barrier((value, *earlier))[0]


def project_kernel(where_ref, src_ref, *refs):
    mine, theirs, out, held, sems = refs[0:4], refs[4:8], refs[8], refs[9], refs[10]
    z, core = where_ref[0], where_ref[1]
    tensors, deep = mine[0].shape[:2]

    def copies(t):
        moves = []
        for pieces, at in ((mine, core), (theirs, 1 - core)):
            start = pl.multiple_of(at * deep, 64)
            rows = pl.ds(start, deep)
            for piece, step in zip(pieces, (0, 3, 1, 2)):
                moves.append((piece.at[t], held.at[t, (z + step) % 4, rows]))
        return [
            pltpu.make_async_copy(src, dst, sems.at[t, n]) for n, (src, dst) in enumerate(moves)
        ]

    t, i = pl.program_id(0), pl.program_id(1)

    @pl.when((t == 0) & (i == 0))
    def _():
        for n in range(tensors):
            for copy in copies(n):
                copy.start()

    @pl.when(i == 0)
    def _():
        for copy in copies(t):
            copy.wait()

    acc = jnp.dot(src_ref[0], held[t, 0], preferred_element_type=F32)
    for n in range(1, 4):
        acc += jnp.dot(src_ref[n], held[t, n], preferred_element_type=F32)
    out[0] = acc.astype(BF)


def project(where, source, mine, theirs):
    rows, depth = source.shape[1:]
    tensors, _, wide = mine[0].shape
    tile = 256
    pieces = [*mine, *theirs]
    return pl.pallas_call(
        project_kernel,
        grid_spec=pltpu.PrefetchScalarGridSpec(
            num_scalar_prefetch=1,
            grid=(tensors, rows // tile),
            in_specs=[
                pl.BlockSpec((4, tile, depth), lambda t, i, where: (0, i, 0)),
                *[pl.BlockSpec(memory_space=pl.ANY) for p in pieces],
            ],
            out_specs=pl.BlockSpec((1, tile, wide), lambda t, i, where: (t, i, 0)),
            scratch_shapes=[
                pltpu.VMEM((tensors, 4, depth, wide), BF),
                pltpu.SemaphoreType.DMA((tensors, 8)),
            ],
        ),
        out_shape=jax.ShapeDtypeStruct((tensors, rows, wide), BF),
        compiler_params=pltpu.CompilerParams(vmem_limit_bytes=26 << 20),
        cost_estimate=pl.CostEstimate(
            flops=2 * rows * 4 * depth * wide * tensors,
            bytes_accessed=2 * rows * (4 * depth + wide * tensors) + 8 * depth * wide * tensors,
            transcendentals=0,
        ),
    )(where, source, *pieces)


STEP = 3


def attend_kernel(flags, query_ref, *refs, fresh, cached, begun, ended):
    refs = list(refs)
    fresh_refs = [refs.pop(0) for _ in range(2 * fresh)]
    cached_refs = [refs.pop(0) for _ in range(2 * cached)]
    state_in = [refs.pop(0) for _ in range(3 * begun)]
    out = refs.pop(0) if ended else None
    state = refs
    factor = math.log2(math.e) / math.sqrt(HS)
    cuts = [slice(h * HS, (h + 1) * HS) for h in range(STEP)]

    def scores(key_ref, h):
        return lax.dot_general(
            key_ref[0, :, cuts[h]],
            query_ref[0, :, cuts[h]],
            (((1,), (1,)), ((), ())),
            preferred_element_type=F32,
        )

    def absorb(key_ref, value_ref, held, kept):
        ahead = scores(key_ref, 0)
        for h in range(STEP):
            s = ahead
            if h + 1 < STEP:
                ahead = scores(key_ref, h + 1)
            top = jnp.max(s, axis=0, keepdims=True)
            if held:
                old = held[0][h, :1]
                top = jnp.maximum(old, top)
            p = jnp.exp2((s - top) * factor)
            total = jnp.sum(p, axis=0, keepdims=True)
            summed = lax.dot_general(
                value_ref[0, :, cuts[h]],
                p.astype(BF),
                (((0,), (0,)), ((), ())),
                preferred_element_type=F32,
            )
            if held:
                scale = jnp.exp2((old - top) * factor)
                total += held[1][h, :1] * scale
                summed += held[2][h] * scale
            if kept:
                kept[0][h, :1] = top
                kept[1][h, :1] = total
                kept[2][h] = summed
            else:
                out[:, cuts[h]] = (summed / total).T.astype(BF)

    if fresh:
        last = ended and not cached
        absorb(*fresh_refs, state_in if begun else None, None if last else state)
    else:
        state[0][...] = jnp.full(state[0].shape, -jnp.inf, F32)
        state[1][...] = jnp.zeros(state[1].shape, F32)
        state[2][...] = jnp.zeros(state[2].shape, F32)
    for n in range(cached):

        @pl.when(flags[n] > 0)
        def _():
            absorb(cached_refs[2 * n], cached_refs[2 * n + 1], state, state)

    if ended and cached:
        for h in range(STEP):
            out[:, cuts[h]] = (state[2][h] / state[1][h, :1]).T.astype(BF)


def attend(flags, query, fresh, cached, groups, state=None, ended=True):
    rows = query.shape[1]
    first, count = groups
    at = lambda n: pl.BlockSpec((1, rows, STEP * HS), lambda g, flags: (n, 0, first + g))
    tall = [(STEP, 8, rows), (STEP, 8, rows), (STEP, HS, rows)]
    state_specs = [pl.BlockSpec(t, lambda g, flags: (first + g, 0, 0)) for t in tall]
    sources = [s for s in (*fresh, *cached) for _ in range(2)]
    blocks = 2 if not cached else 5
    kernel = functools.partial(
        attend_kernel,
        fresh=len(fresh),
        cached=len(cached),
        begun=state is not None,
        ended=ended,
    )
    heads = count * STEP
    return pl.pallas_call(
        kernel,
        grid_spec=pltpu.PrefetchScalarGridSpec(
            num_scalar_prefetch=1,
            grid=(count,),
            in_specs=[at(0)] + [at(0), at(1)] * (len(sources) // 2) + state_specs * (state is not None),
            out_specs=pl.BlockSpec((rows, STEP * HS), lambda g, flags: (0, g)) if ended else state_specs,
            scratch_shapes=[pltpu.VMEM(t, F32) for t in tall] if ended and cached else [],
        ),
        out_shape=jax.ShapeDtypeStruct((rows, heads * HS), BF)
        if ended
        else [jax.ShapeDtypeStruct((heads, *t[1:]), F32) for t in tall],
        compiler_params=pltpu.CompilerParams(vmem_limit_bytes=30 << 20),
        cost_estimate=pl.CostEstimate(
            flops=blocks * 8 * rows * rows * heads * HS,
            bytes_accessed=blocks * 4 * rows * heads * HS,
            transcendentals=blocks * rows * rows * heads,
        ),
    )(flags, query, *sources, *(state or ()))


def body(
    latent, mod_scale, mod_shift, w_query, w_key, w_value, cache_keys, cache_values, block_lists
):
    core, xh = lax.axis_index("c"), lax.axis_index("xh")
    z, y, xl = lax.axis_index("z"), lax.axis_index("y"), lax.axis_index("xl")
    rows = latent.shape[1]
    thin, full = w_query.shape
    wide = full // 2
    even = xl == 0

    def halves(array):
        left, right = array[..., :wide], array[..., wide:]
        return jnp.where(even, left, right), jnp.where(even, right, left)

    def in_order(is_first, mine, theirs, axis):
        return jnp.concatenate(
            [jnp.where(is_first, mine, theirs), jnp.where(is_first, theirs, mine)], axis=axis
        )

    listed = block_lists[0]
    kept, sent = (jnp.stack(arrays) for arrays in zip(*map(halves, (w_query, w_key, w_value))))
    got = permuted(sent, partner)
    (keys_mine, keys_sent), (values_mine, values_sent) = map(halves, (cache_keys[0], cache_values[0]))
    kv_mine = jnp.stack([keys_mine, values_mine])
    near = [permuted(kv_mine, along_pairs(step)) for step in (1, -1)]
    pair = in_order(even, kept, got, 1)
    ring = in_order(xh == 0, pair, permuted(pair, other_half), 1)
    lists = jnp.concatenate([listed, permuted(listed, partner)], axis=0)
    kv_got = permuted(after(jnp.stack([keys_sent, values_sent]), ring, lists), partner)
    ring = after(ring, lists)
    plane = jnp.zeros((3, NY, 4 * thin, wide), BF)
    for step in range(NY):
        piece = permuted(ring, along_y(-step)) if step else ring
        plane = lax.dynamic_update_slice(plane, piece[:, None], (0, (y + step) % NY, 0, 0))
    deep = NY * 4 * thin
    plane = after(plane.reshape(3, deep, wide), *near)

    values_in = latent[0].astype(F32)
    factor = lax.rsqrt(jnp.mean(values_in * values_in, axis=-1, keepdims=True) + 1e-06)
    normed = (values_in * factor * mod_scale[0][None, :] + mod_shift[0][None, :]).astype(BF)
    depth = 2 * deep
    by_z = jnp.transpose(normed.reshape(rows, 4, 4, depth // 4), (2, 0, 1, 3)).reshape(4, rows, depth)
    place = lax.broadcasted_iota(jnp.int32, (depth, depth), 1)
    row = place % thin
    at_xl = place // thin % 2
    at_xh = place // (2 * thin) % 2
    at_y = place // (4 * thin) % 4
    at_c = place // deep
    wanted = (((at_xh * 2 + at_c) * 4 + at_y) * 2 + at_xl) * thin + row
    order = (lax.broadcasted_iota(jnp.int32, (depth, depth), 0) == wanted).astype(BF)
    mine = lax.dot_general(by_z, order, (((2,), (0,)), ((), ())), preferred_element_type=BF)

    where = jnp.stack([z, core]).astype(jnp.int32)
    def z_ring(own):
        return own, *(permuted(own, along_z(step)) for step in (1, -1, 2))

    crossed = lambda value: permuted(value, other_core)
    query_weights = z_ring(plane[:1])
    theirs = permuted(after(mine, kv_got, query_weights[1]), partner)
    fresh_weights = z_ring(after(plane[1:], *query_weights[1:]))
    across = crossed(plane)
    query_theirs = (across[:1], *map(crossed, query_weights[1:]))
    block = (z * NY + y) * 2 + xl
    other = block + jnp.where(even, 1, -1)
    named = jnp.stack([block, other, block - 2, block + 2, other - 2, other + 2])
    flags = jnp.any(lists[:, None, :] == named[None, :, None], axis=-1).astype(jnp.int32)
    cached = (kv_mine, kv_got, *near)

    query = project(where, mine, query_weights, query_theirs)
    state = attend(flags[0, :4], query, (), cached, (0, 2), ended=False)
    late = after(kv_got, *state, *fresh_weights[1:])
    far = [permuted(late, along_pairs(step)) for step in (1, -1)]
    fresh_theirs = (across[1:], *(crossed(after(w, *state)) for w in fresh_weights[1:]))
    their_query = project(where, after(theirs, *state), query_weights, query_theirs)
    their_state = attend(flags[1, :4], their_query, (), cached, (0, 2), ended=False)
    their_fresh = project(where, after(theirs, *their_state), fresh_weights, fresh_theirs)
    fresh = project(where, after(mine, their_fresh), fresh_weights, fresh_theirs)
    their_query = after(their_query, fresh)
    low = attend(flags[1, 4:], their_query, (their_fresh,), far, (0, 1), their_state)
    low_back = permuted(low, partner)
    high = attend(flags[1, 4:], their_query, (their_fresh,), far, (1, 1), their_state)
    high_back = permuted(high, partner)
    own = attend(flags[0, 4:], query, (fresh,), far, (0, 2), state)
    back = jnp.concatenate([low_back, high_back], axis=1)
    return in_order(even, own, back, 1)[None]


def solution(mesh):
    fine = Mesh(mesh.devices.reshape(DIMS), AXES)
    dp, seq = ("xh", "c"), ("z", "y", "xl")
    placed = (
        P(dp, seq, None),
        P(dp, None),
        P(dp, None),
        P(dp + seq, None),
        P(dp + seq, None),
        P(dp + seq, None),
        P(dp, seq, None),
        P(dp, seq, None),
        P(dp, seq, None),
    )
    return jax.shard_map(
        body, mesh=fine, in_specs=placed, out_specs=P(dp, seq, None), check_vma=False
    )
```

```python
import functools
import itertools
import math

import jax
import jax.numpy as jnp
from jax import lax
from jax.experimental import pallas as pl
from jax.experimental.pallas import tpu as pltpu
from jax.sharding import Mesh
from jax.sharding import PartitionSpec as P

HS = 128
NZ, NY = 4, 4
AXES = ("xh", "c", "z", "y", "xl")
DIMS = (2, 2, 4, 4, 2)
BF = jnp.bfloat16
F32 = jnp.float32


def flat(place):
    index = 0
    for at, size in zip(place, DIMS):
        index = index * size + at
    return index


def permuted(value, move):
    places = itertools.product(*(range(n) for n in DIMS))
    moves = ((place, move(*place)) for place in places)
    return lax.ppermute(value, AXES, [(flat(p), flat(q)) for p, q in moves if q is not None])


def other_core(xh, c, z, y, xl):
    return xh, 1 - c, z, y, xl


def other_half(xh, c, z, y, xl):
    return 1 - xh, c, z, y, xl


def partner(xh, c, z, y, xl):
    return xh, c, z, y, 1 - xl


def along_z(step):
    return lambda xh, c, z, y, xl: (xh, c, (z + step) % NZ, y, xl)


def along_y(step):
    return lambda xh, c, z, y, xl: (xh, c, z, (y + step) % NY, xl)


def along_pairs(step):
    def move(xh, c, z, y, xl):
        at = z * NY + y + step
        return (xh, c, at // NY, at % NY, xl) if 0 <= at < NZ * NY else None

    return move


def after(value, *earlier):
    return lax.optimization_barrier((value, *earlier))[0]


def project_kernel(where_ref, src_ref, *refs):
    mine, theirs, out, held, sems = refs[0:4], refs[4:8], refs[8], refs[9], refs[10]
    z, core = where_ref[0], where_ref[1]
    tensors, deep = mine[0].shape[:2]

    def copies(t):
        moves = []
        for pieces, at in ((mine, core), (theirs, 1 - core)):
            start = pl.multiple_of(at * deep, 64)
            rows = pl.ds(start, deep)
            for piece, step in zip(pieces, (0, 3, 1, 2)):
                moves.append((piece.at[t], held.at[t, (z + step) % 4, rows]))
        return [
            pltpu.make_async_copy(src, dst, sems.at[t, n]) for n, (src, dst) in enumerate(moves)
        ]

    t, i = pl.program_id(0), pl.program_id(1)

    @pl.when((t == 0) & (i == 0))
    def _():
        for n in range(tensors):
            for copy in copies(n):
                copy.start()

    @pl.when(i == 0)
    def _():
        for copy in copies(t):
            copy.wait()

    acc = jnp.dot(src_ref[0], held[t, 0], preferred_element_type=F32)
    for n in range(1, 4):
        acc += jnp.dot(src_ref[n], held[t, n], preferred_element_type=F32)
    out[0] = acc.astype(BF)


def project(where, source, mine, theirs):
    rows, depth = source.shape[1:]
    tensors, _, wide = mine[0].shape
    tile = 512
    pieces = [*mine, *theirs]
    return pl.pallas_call(
        project_kernel,
        grid_spec=pltpu.PrefetchScalarGridSpec(
            num_scalar_prefetch=1,
            grid=(tensors, rows // tile),
            in_specs=[
                pl.BlockSpec((4, tile, depth), lambda t, i, where: (0, i, 0)),
                *[pl.BlockSpec(memory_space=pl.ANY) for p in pieces],
            ],
            out_specs=pl.BlockSpec((1, tile, wide), lambda t, i, where: (t, i, 0)),
            scratch_shapes=[
                pltpu.VMEM((tensors, 4, depth, wide), BF),
                pltpu.SemaphoreType.DMA((tensors, 8)),
            ],
        ),
        out_shape=jax.ShapeDtypeStruct((tensors, rows, wide), BF),
        compiler_params=pltpu.CompilerParams(vmem_limit_bytes=26 << 20),
        cost_estimate=pl.CostEstimate(
            flops=2 * rows * 4 * depth * wide * tensors,
            bytes_accessed=2 * rows * (4 * depth + wide * tensors) + 8 * depth * wide * tensors,
            transcendentals=0,
        ),
    )(where, source, *pieces)


STEP = 3


def attend_kernel(flags, query_ref, *refs, fresh, cached, begun, ended):
    refs = list(refs)
    fresh_refs = [refs.pop(0) for _ in range(2 * fresh)]
    cached_refs = [refs.pop(0) for _ in range(2 * cached)]
    state_in = [refs.pop(0) for _ in range(3 * begun)]
    out = refs.pop(0) if ended else None
    state = refs
    factor = math.log2(math.e) / math.sqrt(HS)
    cuts = [slice(h * HS, (h + 1) * HS) for h in range(STEP)]

    def scores(key_ref, h):
        return lax.dot_general(
            key_ref[0, :, cuts[h]],
            query_ref[0, :, cuts[h]],
            (((1,), (1,)), ((), ())),
            preferred_element_type=F32,
        )

    def absorb(key_ref, value_ref, held, kept):
        ahead = scores(key_ref, 0)
        for h in range(STEP):
            s = ahead
            if h + 1 < STEP:
                ahead = scores(key_ref, h + 1)
            top = jnp.max(s, axis=0, keepdims=True)
            if held:
                old = held[0][h, :1]
                top = jnp.maximum(old, top)
            p = jnp.exp2((s - top) * factor)
            total = jnp.sum(p, axis=0, keepdims=True)
            summed = lax.dot_general(
                value_ref[0, :, cuts[h]],
                p.astype(BF),
                (((0,), (0,)), ((), ())),
                preferred_element_type=F32,
            )
            if held:
                scale = jnp.exp2((old - top) * factor)
                total += held[1][h, :1] * scale
                summed += held[2][h] * scale
            if kept:
                kept[0][h, :1] = top
                kept[1][h, :1] = total
                kept[2][h] = summed
            else:
                out[:, cuts[h]] = (summed / total).T.astype(BF)

    if fresh:
        last = ended and not cached
        absorb(*fresh_refs, state_in if begun else None, None if last else state)
    else:
        state[0][...] = jnp.full(state[0].shape, -jnp.inf, F32)
        state[1][...] = jnp.zeros(state[1].shape, F32)
        state[2][...] = jnp.zeros(state[2].shape, F32)
    for n in range(cached):

        @pl.when(flags[n] > 0)
        def _():
            absorb(cached_refs[2 * n], cached_refs[2 * n + 1], state, state)

    if ended and cached:
        for h in range(STEP):
            out[:, cuts[h]] = (state[2][h] / state[1][h, :1]).T.astype(BF)


def attend(flags, query, fresh, cached, groups, state=None, ended=True):
    rows = query.shape[1]
    first, count = groups
    at = lambda n: pl.BlockSpec((1, rows, STEP * HS), lambda g, flags: (n, 0, first + g))
    tall = [(STEP, 8, rows), (STEP, 8, rows), (STEP, HS, rows)]
    state_specs = [pl.BlockSpec(t, lambda g, flags: (first + g, 0, 0)) for t in tall]
    apart = [isinstance(source, tuple) for source in (*fresh, *cached)]
    sources = [s for source in (*fresh, *cached) for s in (source if isinstance(source, tuple) else (source,) * 2)]
    places = [at(0)] + [spec for two in apart for spec in (at(0), at(0 if two else 1))]
    blocks = 2 if not cached else 5
    kernel = functools.partial(
        attend_kernel,
        fresh=len(fresh),
        cached=len(cached),
        begun=state is not None,
        ended=ended,
    )
    heads = count * STEP
    return pl.pallas_call(
        kernel,
        grid_spec=pltpu.PrefetchScalarGridSpec(
            num_scalar_prefetch=1,
            grid=(count,),
            in_specs=places + state_specs * (state is not None),
            out_specs=pl.BlockSpec((rows, STEP * HS), lambda g, flags: (0, g)) if ended else state_specs,
            scratch_shapes=[pltpu.VMEM(t, F32) for t in tall] if ended and cached else [],
        ),
        out_shape=jax.ShapeDtypeStruct((rows, heads * HS), BF)
        if ended
        else [jax.ShapeDtypeStruct((heads, *t[1:]), F32) for t in tall],
        compiler_params=pltpu.CompilerParams(vmem_limit_bytes=30 << 20),
        cost_estimate=pl.CostEstimate(
            flops=blocks * 8 * rows * rows * heads * HS,
            bytes_accessed=blocks * 4 * rows * heads * HS,
            transcendentals=blocks * rows * rows * heads,
        ),
    )(flags, query, *sources, *(state or ()))


def body(
    latent, mod_scale, mod_shift, w_query, w_key, w_value, cache_keys, cache_values, block_lists
):
    core, xh = lax.axis_index("c"), lax.axis_index("xh")
    z, y, xl = lax.axis_index("z"), lax.axis_index("y"), lax.axis_index("xl")
    rows = latent.shape[1]
    thin, full = w_query.shape
    wide = full // 2
    even = xl == 0

    def halves(array):
        left, right = array[..., :wide], array[..., wide:]
        return jnp.where(even, left, right), jnp.where(even, right, left)

    def in_order(is_first, mine, theirs, axis):
        return jnp.concatenate(
            [jnp.where(is_first, mine, theirs), jnp.where(is_first, theirs, mine)], axis=axis
        )

    listed = block_lists[0]
    kept, sent = (jnp.stack(arrays) for arrays in zip(*map(halves, (w_query, w_key, w_value))))
    got = permuted(sent, partner)
    (keys_mine, keys_sent), (values_mine, values_sent) = map(halves, (cache_keys[0], cache_values[0]))
    kv_mine = jnp.stack([keys_mine, values_mine])
    near_keys = [permuted(kv_mine[:1], along_pairs(step)) for step in (1, -1)]
    pair = in_order(even, kept, got, 1)
    ring = in_order(xh == 0, pair, permuted(pair, other_half), 1)
    lists = jnp.concatenate([listed, permuted(listed, partner)], axis=0)
    kv_got = permuted(after(jnp.stack([keys_sent, values_sent]), ring, lists), partner)
    ring = after(ring, lists)
    plane = jnp.zeros((3, NY, 4 * thin, wide), BF)
    before, behind = permuted(ring, along_y(1)), permuted(ring, along_y(-1))
    pieces = (ring, behind, permuted(before, along_y(1)), before)
    for step, piece in enumerate(pieces):
        plane = lax.dynamic_update_slice(plane, piece[:, None], (0, (y + step) % NY, 0, 0))
    deep = NY * 4 * thin
    plane = after(plane.reshape(3, deep, wide), *near_keys)

    values_in = after(latent[0], got).astype(F32)
    factor = lax.rsqrt(jnp.mean(values_in * values_in, axis=-1, keepdims=True) + 1e-06)
    normed = (values_in * factor * mod_scale[0][None, :] + mod_shift[0][None, :]).astype(BF)
    depth = 2 * deep
    by_z = jnp.transpose(normed.reshape(rows, 4, 4, depth // 4), (2, 0, 1, 3)).reshape(4, rows, depth)
    place = lax.broadcasted_iota(jnp.int32, (depth, depth), 1)
    row = place % thin
    at_xl = place // thin % 2
    at_xh = place // (2 * thin) % 2
    at_y = place // (4 * thin) % 4
    at_c = place // deep
    wanted = (((at_xh * 2 + at_c) * 4 + at_y) * 2 + at_xl) * thin + row
    order = (lax.broadcasted_iota(jnp.int32, (depth, depth), 0) == wanted).astype(BF)
    mine = lax.dot_general(by_z, order, (((2,), (0,)), ((), ())), preferred_element_type=BF)

    where = jnp.stack([z, core]).astype(jnp.int32)
    def along_z_ring(own, steps):
        return own, *(permuted(own, along_z(step)) for step in steps)

    crossed = lambda value: permuted(value, other_core)
    query_weights = along_z_ring(plane[:1], (1, -1, 2))
    theirs = permuted(after(mine, kv_got, *query_weights[1:]), partner)
    fresh_weights = along_z_ring(after(plane[1:], *query_weights[1:]), (1, -1))
    late = after(kv_mine[1:], *query_weights[1:])
    near_values = [permuted(late, along_pairs(step)) for step in (1, -1)]
    across = crossed(plane)
    query_theirs = (across[:1], *map(crossed, query_weights[1:]))

    block = (z * NY + y) * 2 + xl
    other = block + jnp.where(even, 1, -1)
    named = jnp.stack([block, other, block - 2, block + 2, other - 2, other + 2])
    flags = jnp.any(lists[:, None, :] == named[None, :, None], axis=-1).astype(jnp.int32)
    cached = (kv_mine, kv_got, *zip(near_keys, near_values))

    query = project(where, mine, query_weights, query_theirs)
    state = attend(flags[0, :4], query, (), cached, (0, 2), ended=False)
    half = deep // 2
    below, above = after(fresh_weights[1:], *state)
    top = permuted(below[:, :half], along_z(1))
    bottom = permuted(above[:, half:], along_z(-1))
    fresh_weights = (*fresh_weights, jnp.concatenate([top, bottom], axis=1))
    late = after(kv_got, top, bottom)
    far = [permuted(late, along_pairs(step)) for step in (1, -1)]
    fresh_theirs = (across[1:], *(crossed(after(w, *state)) for w in fresh_weights[1:]))
    their_query = project(where, after(theirs, *state), query_weights, query_theirs)
    their_state = attend(flags[1, :4], their_query, (), cached, (0, 2), ended=False)
    their_fresh = project(where, after(theirs, *their_state), fresh_weights, fresh_theirs)
    fresh = project(where, after(mine, their_fresh), fresh_weights, fresh_theirs)
    low = attend(flags[1, 4:], their_query, (their_fresh,), far, (0, 1), their_state)
    low_back = permuted(low, partner)
    high = attend(flags[1, 4:], their_query, (their_fresh,), far, (1, 1), their_state)
    high_back = permuted(high, partner)
    own = attend(flags[0, 4:], query, (fresh,), far, (0, 2), state)
    back = jnp.concatenate([low_back, high_back], axis=1)
    return in_order(even, own, back, 1)[None]


def solution(mesh):
    fine = Mesh(mesh.devices.reshape(DIMS), AXES)
    dp, seq = ("xh", "c"), ("z", "y", "xl")
    placed = (
        P(dp, seq, None),
        P(dp, None),
        P(dp, None),
        P(dp + seq, None),
        P(dp + seq, None),
        P(dp + seq, None),
        P(dp, seq, None),
        P(dp, seq, None),
        P(dp, seq, None),
    )
    return jax.shard_map(
        body, mesh=fine, in_specs=placed, out_specs=P(dp, seq, None), check_vma=False
    )
```

```python
import functools
import itertools
import math

import jax
import jax.numpy as jnp
from jax import lax
from jax.experimental import pallas as pl
from jax.experimental.pallas import tpu as pltpu
from jax.sharding import Mesh
from jax.sharding import PartitionSpec as P

HS = 128
NZ, NY = 4, 4
AXES = ("xh", "c", "z", "y", "xl")
DIMS = (2, 2, 4, 4, 2)
BF = jnp.bfloat16
F32 = jnp.float32


def flat(place):
    index = 0
    for at, size in zip(place, DIMS):
        index = index * size + at
    return index


def permuted(value, move):
    places = itertools.product(*(range(n) for n in DIMS))
    moves = ((place, move(*place)) for place in places)
    return lax.ppermute(value, AXES, [(flat(p), flat(q)) for p, q in moves if q is not None])


def other_core(xh, c, z, y, xl):
    return xh, 1 - c, z, y, xl


def other_half(xh, c, z, y, xl):
    return 1 - xh, c, z, y, xl


def partner(xh, c, z, y, xl):
    return xh, c, z, y, 1 - xl


def along_z(step):
    return lambda xh, c, z, y, xl: (xh, c, (z + step) % NZ, y, xl)


def along_y(step):
    return lambda xh, c, z, y, xl: (xh, c, z, (y + step) % NY, xl)


def along_pairs(step):
    def move(xh, c, z, y, xl):
        at = z * NY + y + step
        return (xh, c, at // NY, at % NY, xl) if 0 <= at < NZ * NY else None

    return move


def after(value, *earlier):
    return lax.optimization_barrier((value, *earlier))[0]


def project_kernel(where_ref, src_ref, *refs):
    mine, theirs, out, held, sems = refs[0:4], refs[4:8], refs[8], refs[9], refs[10]
    z, core = where_ref[0], where_ref[1]
    tensors, deep = mine[0].shape[:2]

    def copies(t):
        moves = []
        for pieces, at in ((mine, core), (theirs, 1 - core)):
            start = pl.multiple_of(at * deep, 64)
            rows = pl.ds(start, deep)
            for piece, step in zip(pieces, (0, 3, 1, 2)):
                moves.append((piece.at[t], held.at[t, (z + step) % 4, rows]))
        return [
            pltpu.make_async_copy(src, dst, sems.at[t, n]) for n, (src, dst) in enumerate(moves)
        ]

    t, i = pl.program_id(0), pl.program_id(1)

    @pl.when((t == 0) & (i == 0))
    def _():
        for n in range(tensors):
            for copy in copies(n):
                copy.start()

    @pl.when(i == 0)
    def _():
        for copy in copies(t):
            copy.wait()

    acc = jnp.dot(src_ref[0], held[t, 0], preferred_element_type=F32)
    for n in range(1, 4):
        acc += jnp.dot(src_ref[n], held[t, n], preferred_element_type=F32)
    out[0] = acc.astype(BF)


def project(where, source, mine, theirs):
    rows, depth = source.shape[1:]
    tensors, _, wide = mine[0].shape
    tile = 512
    pieces = [*mine, *theirs]
    return pl.pallas_call(
        project_kernel,
        grid_spec=pltpu.PrefetchScalarGridSpec(
            num_scalar_prefetch=1,
            grid=(tensors, rows // tile),
            in_specs=[
                pl.BlockSpec((4, tile, depth), lambda t, i, where: (0, i, 0)),
                *[pl.BlockSpec(memory_space=pl.ANY) for p in pieces],
            ],
            out_specs=pl.BlockSpec((1, tile, wide), lambda t, i, where: (t, i, 0)),
            scratch_shapes=[
                pltpu.VMEM((tensors, 4, depth, wide), BF),
                pltpu.SemaphoreType.DMA((tensors, 8)),
            ],
        ),
        out_shape=jax.ShapeDtypeStruct((tensors, rows, wide), BF),
        compiler_params=pltpu.CompilerParams(vmem_limit_bytes=26 << 20),
        cost_estimate=pl.CostEstimate(
            flops=2 * rows * 4 * depth * wide * tensors,
            bytes_accessed=2 * rows * (4 * depth + wide * tensors) + 8 * depth * wide * tensors,
            transcendentals=0,
        ),
    )(where, source, *pieces)


STEP = 3


def attend_kernel(flags, query_ref, *refs, fresh, cached, begun, ended):
    refs = list(refs)
    fresh_refs = [refs.pop(0) for _ in range(2 * fresh)]
    cached_refs = [refs.pop(0) for _ in range(2 * cached)]
    state_in = [refs.pop(0) for _ in range(3 * begun)]
    out = refs.pop(0) if ended else None
    state = refs
    factor = math.log2(math.e) / math.sqrt(HS)
    cuts = [slice(h * HS, (h + 1) * HS) for h in range(STEP)]

    def scores(key_ref, h):
        return lax.dot_general(
            key_ref[0, :, cuts[h]],
            query_ref[0, :, cuts[h]],
            (((1,), (1,)), ((), ())),
            preferred_element_type=F32,
        )

    def absorb(key_ref, value_ref, held, kept):
        ahead = scores(key_ref, 0)
        for h in range(STEP):
            s = ahead
            if h + 1 < STEP:
                ahead = scores(key_ref, h + 1)
            top = jnp.max(s, axis=0, keepdims=True)
            if held:
                old = held[0][h, :1]
                top = jnp.maximum(old, top)
            p = jnp.exp2((s - top) * factor)
            total = jnp.sum(p, axis=0, keepdims=True)
            summed = lax.dot_general(
                value_ref[0, :, cuts[h]],
                p.astype(BF),
                (((0,), (0,)), ((), ())),
                preferred_element_type=F32,
            )
            if held:
                scale = jnp.exp2((old - top) * factor)
                total += held[1][h, :1] * scale
                summed += held[2][h] * scale
            if kept:
                kept[0][h, :1] = top
                kept[1][h, :1] = total
                kept[2][h] = summed
            else:
                out[:, cuts[h]] = (summed / total).T.astype(BF)

    if fresh:
        last = ended and not cached
        absorb(*fresh_refs, state_in if begun else None, None if last else state)
    else:
        state[0][...] = jnp.full(state[0].shape, -jnp.inf, F32)
        state[1][...] = jnp.zeros(state[1].shape, F32)
        state[2][...] = jnp.zeros(state[2].shape, F32)
    for n in range(cached):

        @pl.when(flags[n] > 0)
        def _():
            absorb(cached_refs[2 * n], cached_refs[2 * n + 1], state, state)

    if ended and cached:
        for h in range(STEP):
            out[:, cuts[h]] = (state[2][h] / state[1][h, :1]).T.astype(BF)


def attend(flags, query, fresh, cached, groups, state=None, ended=True):
    rows = query.shape[1]
    first, count = groups
    at = lambda n: pl.BlockSpec((1, rows, STEP * HS), lambda g, flags: (n, 0, first + g))
    tall = [(STEP, 8, rows), (STEP, 8, rows), (STEP, HS, rows)]
    state_specs = [pl.BlockSpec(t, lambda g, flags: (first + g, 0, 0)) for t in tall]
    apart = [isinstance(source, tuple) for source in (*fresh, *cached)]
    sources = [s for source in (*fresh, *cached) for s in (source if isinstance(source, tuple) else (source,) * 2)]
    places = [at(0)] + [spec for two in apart for spec in (at(0), at(0 if two else 1))]
    blocks = 2 if not cached else 5
    kernel = functools.partial(
        attend_kernel,
        fresh=len(fresh),
        cached=len(cached),
        begun=state is not None,
        ended=ended,
    )
    heads = count * STEP
    return pl.pallas_call(
        kernel,
        grid_spec=pltpu.PrefetchScalarGridSpec(
            num_scalar_prefetch=1,
            grid=(count,),
            in_specs=places + state_specs * (state is not None),
            out_specs=pl.BlockSpec((rows, STEP * HS), lambda g, flags: (0, g)) if ended else state_specs,
            scratch_shapes=[pltpu.VMEM(t, F32) for t in tall] if ended and cached else [],
        ),
        out_shape=jax.ShapeDtypeStruct((rows, heads * HS), BF)
        if ended
        else [jax.ShapeDtypeStruct((heads, *t[1:]), F32) for t in tall],
        compiler_params=pltpu.CompilerParams(vmem_limit_bytes=30 << 20),
        cost_estimate=pl.CostEstimate(
            flops=blocks * 8 * rows * rows * heads * HS,
            bytes_accessed=blocks * 4 * rows * heads * HS,
            transcendentals=blocks * rows * rows * heads,
        ),
    )(flags, query, *sources, *(state or ()))


def body(
    latent, mod_scale, mod_shift, w_query, w_key, w_value, cache_keys, cache_values, block_lists
):
    core, xh = lax.axis_index("c"), lax.axis_index("xh")
    z, y, xl = lax.axis_index("z"), lax.axis_index("y"), lax.axis_index("xl")
    rows = latent.shape[1]
    thin, full = w_query.shape
    wide = full // 2
    even = xl == 0

    def halves(array):
        left, right = array[..., :wide], array[..., wide:]
        return jnp.where(even, left, right), jnp.where(even, right, left)

    def in_order(is_first, mine, theirs, axis):
        return jnp.concatenate(
            [jnp.where(is_first, mine, theirs), jnp.where(is_first, theirs, mine)], axis=axis
        )

    listed = block_lists[0]
    kept, sent = (jnp.stack(arrays) for arrays in zip(*map(halves, (w_query, w_key, w_value))))
    got = permuted(sent, partner)
    (keys_mine, keys_sent), (values_mine, values_sent) = map(halves, (cache_keys[0], cache_values[0]))
    kv_mine = jnp.stack([keys_mine, values_mine])
    near_keys = [permuted(kv_mine[:1], along_pairs(step)) for step in (1, -1)]
    pair = in_order(even, kept, got, 1)
    ring = in_order(xh == 0, pair, permuted(pair, other_half), 1)
    lists = jnp.concatenate([listed, permuted(listed, partner)], axis=0)
    ring = after(ring, lists)
    plane = jnp.zeros((3, NY, 4 * thin, wide), BF)
    before, behind = permuted(ring, along_y(1)), permuted(ring, along_y(-1))
    pieces = (ring, behind, permuted(before, along_y(1)), before)
    for step, piece in enumerate(pieces):
        plane = lax.dynamic_update_slice(plane, piece[:, None], (0, (y + step) % NY, 0, 0))
    deep = NY * 4 * thin
    plane = after(plane.reshape(3, deep, wide), *near_keys)

    values_in = after(latent[0], got).astype(F32)
    factor = lax.rsqrt(jnp.mean(values_in * values_in, axis=-1, keepdims=True) + 1e-06)
    normed = (values_in * factor * mod_scale[0][None, :] + mod_shift[0][None, :]).astype(BF)
    depth = 2 * deep
    by_z = jnp.transpose(normed.reshape(rows, 4, 4, depth // 4), (2, 0, 1, 3)).reshape(4, rows, depth)
    place = lax.broadcasted_iota(jnp.int32, (depth, depth), 1)
    row = place % thin
    at_xl = place // thin % 2
    at_xh = place // (2 * thin) % 2
    at_y = place // (4 * thin) % 4
    at_c = place // deep
    wanted = (((at_xh * 2 + at_c) * 4 + at_y) * 2 + at_xl) * thin + row
    order = (lax.broadcasted_iota(jnp.int32, (depth, depth), 0) == wanted).astype(BF)
    mine = lax.dot_general(by_z, order, (((2,), (0,)), ((), ())), preferred_element_type=BF)
    theirs = permuted(after(mine, lists, ring), partner)
    kv_got = permuted(after(jnp.stack([keys_sent, values_sent]), theirs), partner)

    where = jnp.stack([z, core]).astype(jnp.int32)
    def along_z_ring(own, steps):
        return own, *(permuted(own, along_z(step)) for step in steps)

    crossed = lambda value: permuted(value, other_core)
    query_weights = along_z_ring(plane[:1], (1, -1, 2))
    fresh_weights = along_z_ring(after(plane[1:], *query_weights[1:]), (1, -1))
    late = after(kv_mine[1:], *query_weights[1:])
    near_values = [permuted(late, along_pairs(step)) for step in (1, -1)]
    across = crossed(plane)
    query_theirs = (across[:1], *map(crossed, query_weights[1:]))

    block = (z * NY + y) * 2 + xl
    other = block + jnp.where(even, 1, -1)
    named = jnp.stack([block, other, block - 2, block + 2, other - 2, other + 2])
    flags = jnp.any(lists[:, None, :] == named[None, :, None], axis=-1).astype(jnp.int32)
    cached = (kv_mine, kv_got, *zip(near_keys, near_values))

    query = project(where, mine, query_weights, query_theirs)
    state = attend(flags[0, :4], query, (), cached, (0, 2), ended=False)
    their_query = project(where, after(theirs, query), query_weights, query_theirs)
    half = deep // 2
    below, above = after(fresh_weights[1:], query)
    top = permuted(below[:, :half], along_z(1))
    bottom = permuted(above[:, half:], along_z(-1))
    fresh_weights = (*fresh_weights, jnp.concatenate([top, bottom], axis=1))
    late = after(kv_got, top, bottom)
    far = [permuted(late, along_pairs(step)) for step in (1, -1)]
    fresh_theirs = (across[1:], *(crossed(after(w, their_query)) for w in fresh_weights[1:]))
    their_state = attend(flags[1, :4], their_query, (), cached, (0, 2), ended=False)
    their_fresh = project(where, after(theirs, *their_state), fresh_weights, fresh_theirs)
    fresh = project(where, after(mine, their_fresh), fresh_weights, fresh_theirs)
    low = attend(flags[1, 4:], their_query, (their_fresh,), far, (0, 1), their_state)
    low_back = permuted(low, partner)
    high = attend(flags[1, 4:], their_query, (their_fresh,), far, (1, 1), their_state)
    high_back = permuted(high, partner)
    own = attend(flags[0, 4:], query, (fresh,), far, (0, 2), state)
    back = jnp.concatenate([low_back, high_back], axis=1)
    return in_order(even, own, back, 1)[None]


def solution(mesh):
    fine = Mesh(mesh.devices.reshape(DIMS), AXES)
    dp, seq = ("xh", "c"), ("z", "y", "xl")
    placed = (
        P(dp, seq, None),
        P(dp, None),
        P(dp, None),
        P(dp + seq, None),
        P(dp + seq, None),
        P(dp + seq, None),
        P(dp, seq, None),
        P(dp, seq, None),
        P(dp, seq, None),
    )
    return jax.shard_map(
        body, mesh=fine, in_specs=placed, out_specs=P(dp, seq, None), check_vma=False
    )
```

```python
import functools
import itertools
import math

import jax
import jax.numpy as jnp
from jax import lax
from jax.experimental import pallas as pl
from jax.experimental.pallas import tpu as pltpu
from jax.sharding import Mesh
from jax.sharding import PartitionSpec as P

HS = 128
NZ, NY = 4, 4
AXES = ("xh", "c", "z", "y", "xl")
DIMS = (2, 2, 4, 4, 2)
BF = jnp.bfloat16
F32 = jnp.float32


def flat(place):
    index = 0
    for at, size in zip(place, DIMS):
        index = index * size + at
    return index


def permuted(value, move):
    places = itertools.product(*(range(n) for n in DIMS))
    moves = ((place, move(*place)) for place in places)
    return lax.ppermute(value, AXES, [(flat(p), flat(q)) for p, q in moves if q is not None])


def other_core(xh, c, z, y, xl):
    return xh, 1 - c, z, y, xl


def other_half(xh, c, z, y, xl):
    return 1 - xh, c, z, y, xl


def partner(xh, c, z, y, xl):
    return xh, c, z, y, 1 - xl


def along_z(step):
    return lambda xh, c, z, y, xl: (xh, c, (z + step) % NZ, y, xl)


def along_y(step):
    return lambda xh, c, z, y, xl: (xh, c, z, (y + step) % NY, xl)


def along_pairs(step):
    def move(xh, c, z, y, xl):
        at = z * NY + y + step
        return (xh, c, at // NY, at % NY, xl) if 0 <= at < NZ * NY else None

    return move


def after(value, *earlier):
    return lax.optimization_barrier((value, *earlier))[0]


def project_kernel(where_ref, *refs, count):
    sources, refs = refs[:count], refs[count:]
    mine, theirs, outs = refs[0:4], refs[4:8], refs[8 : 8 + count]
    held, sems = refs[8 + count :]
    z, core = where_ref[0], where_ref[1]
    tensors, deep = mine[0].shape[:2]

    def copies(t):
        moves = []
        for pieces, at in ((mine, core), (theirs, 1 - core)):
            start = pl.multiple_of(at * deep, 64)
            rows = pl.ds(start, deep)
            for piece, step in zip(pieces, (0, 3, 1, 2)):
                moves.append((piece.at[t], held.at[t, (z + step) % 4, rows]))
        return [
            pltpu.make_async_copy(src, dst, sems.at[t, n]) for n, (src, dst) in enumerate(moves)
        ]

    t, i = pl.program_id(0), pl.program_id(1)

    @pl.when((t == 0) & (i == 0))
    def _():
        for n in range(tensors):
            for copy in copies(n):
                copy.start()

    @pl.when(i == 0)
    def _():
        for copy in copies(t):
            copy.wait()

    for src_ref, out in zip(sources, outs):
        acc = jnp.dot(src_ref[0], held[t, 0], preferred_element_type=F32)
        for n in range(1, 4):
            acc += jnp.dot(src_ref[n], held[t, n], preferred_element_type=F32)
        out[0] = acc.astype(BF)


def project(where, sources, mine, theirs):
    count = len(sources)
    rows, depth = sources[0].shape[1:]
    tensors, _, wide = mine[0].shape
    tile = 512
    pieces = [*mine, *theirs]
    return pl.pallas_call(
        functools.partial(project_kernel, count=count),
        grid_spec=pltpu.PrefetchScalarGridSpec(
            num_scalar_prefetch=1,
            grid=(tensors, rows // tile),
            in_specs=[
                *[pl.BlockSpec((4, tile, depth), lambda t, i, where: (0, i, 0))] * count,
                *[pl.BlockSpec(memory_space=pl.ANY) for p in pieces],
            ],
            out_specs=[pl.BlockSpec((1, tile, wide), lambda t, i, where: (t, i, 0))] * count,
            scratch_shapes=[
                pltpu.VMEM((tensors, 4, depth, wide), BF),
                pltpu.SemaphoreType.DMA((tensors, 8)),
            ],
        ),
        out_shape=[jax.ShapeDtypeStruct((tensors, rows, wide), BF)] * count,
        compiler_params=pltpu.CompilerParams(vmem_limit_bytes=32 << 20),
        cost_estimate=pl.CostEstimate(
            flops=2 * count * rows * 4 * depth * wide * tensors,
            bytes_accessed=2 * count * rows * (4 * depth + wide * tensors) + 8 * depth * wide * tensors,
            transcendentals=0,
        ),
    )(where, *sources, *pieces)


STEP = 3


def attend_kernel(flags, query_ref, *refs, fresh, cached, begun, ended):
    refs = list(refs)
    fresh_refs = [refs.pop(0) for _ in range(2 * fresh)]
    cached_refs = [refs.pop(0) for _ in range(2 * cached)]
    state_in = [refs.pop(0) for _ in range(3 * begun)]
    out = refs.pop(0) if ended else None
    state = refs
    factor = math.log2(math.e) / math.sqrt(HS)
    cuts = [slice(h * HS, (h + 1) * HS) for h in range(STEP)]

    def scores(key_ref, h):
        return lax.dot_general(
            key_ref[0, :, cuts[h]],
            query_ref[0, :, cuts[h]],
            (((1,), (1,)), ((), ())),
            preferred_element_type=F32,
        )

    def absorb(key_ref, value_ref, held, kept):
        ahead = scores(key_ref, 0)
        for h in range(STEP):
            s = ahead
            if h + 1 < STEP:
                ahead = scores(key_ref, h + 1)
            top = jnp.max(s, axis=0, keepdims=True)
            if held:
                old = held[0][h, :1]
                top = jnp.maximum(old, top)
            p = jnp.exp2((s - top) * factor)
            total = jnp.sum(p, axis=0, keepdims=True)
            summed = lax.dot_general(
                value_ref[0, :, cuts[h]],
                p.astype(BF),
                (((0,), (0,)), ((), ())),
                preferred_element_type=F32,
            )
            if held:
                scale = jnp.exp2((old - top) * factor)
                total += held[1][h, :1] * scale
                summed += held[2][h] * scale
            if kept:
                kept[0][h, :1] = top
                kept[1][h, :1] = total
                kept[2][h] = summed
            else:
                out[:, cuts[h]] = (summed / total).T.astype(BF)

    if fresh:
        last = ended and not cached
        absorb(*fresh_refs, state_in if begun else None, None if last else state)
    else:
        state[0][...] = jnp.full(state[0].shape, -jnp.inf, F32)
        state[1][...] = jnp.zeros(state[1].shape, F32)
        state[2][...] = jnp.zeros(state[2].shape, F32)
    for n in range(cached):

        @pl.when(flags[n] > 0)
        def _():
            absorb(cached_refs[2 * n], cached_refs[2 * n + 1], state, state)

    if ended and cached:
        for h in range(STEP):
            out[:, cuts[h]] = (state[2][h] / state[1][h, :1]).T.astype(BF)


def attend(flags, query, fresh, cached, groups, state=None, ended=True):
    rows = query.shape[1]
    first, count = groups
    at = lambda n: pl.BlockSpec((1, rows, STEP * HS), lambda g, flags: (n, 0, first + g))
    tall = [(STEP, 8, rows), (STEP, 8, rows), (STEP, HS, rows)]
    state_specs = [pl.BlockSpec(t, lambda g, flags: (first + g, 0, 0)) for t in tall]
    apart = [isinstance(source, tuple) for source in (*fresh, *cached)]
    sources = [s for source in (*fresh, *cached) for s in (source if isinstance(source, tuple) else (source,) * 2)]
    places = [at(0)] + [spec for two in apart for spec in (at(0), at(0 if two else 1))]
    blocks = 2 if not cached else 5
    kernel = functools.partial(
        attend_kernel,
        fresh=len(fresh),
        cached=len(cached),
        begun=state is not None,
        ended=ended,
    )
    heads = count * STEP
    return pl.pallas_call(
        kernel,
        grid_spec=pltpu.PrefetchScalarGridSpec(
            num_scalar_prefetch=1,
            grid=(count,),
            in_specs=places + state_specs * (state is not None),
            out_specs=pl.BlockSpec((rows, STEP * HS), lambda g, flags: (0, g)) if ended else state_specs,
            scratch_shapes=[pltpu.VMEM(t, F32) for t in tall] if ended and cached else [],
        ),
        out_shape=jax.ShapeDtypeStruct((rows, heads * HS), BF)
        if ended
        else [jax.ShapeDtypeStruct((heads, *t[1:]), F32) for t in tall],
        compiler_params=pltpu.CompilerParams(vmem_limit_bytes=30 << 20),
        cost_estimate=pl.CostEstimate(
            flops=blocks * 8 * rows * rows * heads * HS,
            bytes_accessed=blocks * 4 * rows * heads * HS,
            transcendentals=blocks * rows * rows * heads,
        ),
    )(flags, query, *sources, *(state or ()))


def body(
    latent, mod_scale, mod_shift, w_query, w_key, w_value, cache_keys, cache_values, block_lists
):
    core, xh = lax.axis_index("c"), lax.axis_index("xh")
    z, y, xl = lax.axis_index("z"), lax.axis_index("y"), lax.axis_index("xl")
    rows = latent.shape[1]
    thin, full = w_query.shape
    wide = full // 2
    even = xl == 0

    def halves(array):
        left, right = array[..., :wide], array[..., wide:]
        return jnp.where(even, left, right), jnp.where(even, right, left)

    def in_order(is_first, mine, theirs, axis):
        return jnp.concatenate(
            [jnp.where(is_first, mine, theirs), jnp.where(is_first, theirs, mine)], axis=axis
        )

    listed = block_lists[0]
    kept, sent = (jnp.stack(arrays) for arrays in zip(*map(halves, (w_query, w_key, w_value))))
    got = permuted(sent, partner)
    (keys_mine, keys_sent), (values_mine, values_sent) = map(halves, (cache_keys[0], cache_values[0]))
    kv_mine = jnp.stack([keys_mine, values_mine])
    near_keys = [permuted(kv_mine[:1], along_pairs(step)) for step in (1, -1)]
    pair = in_order(even, kept, got, 1)
    ring = in_order(xh == 0, pair, permuted(pair, other_half), 1)
    lists = jnp.concatenate([listed, permuted(listed, partner)], axis=0)
    ring = after(ring, lists)
    plane = jnp.zeros((3, NY, 4 * thin, wide), BF)
    before, behind = permuted(ring, along_y(1)), permuted(ring, along_y(-1))
    pieces = (ring, behind, permuted(before, along_y(1)), before)
    for step, piece in enumerate(pieces):
        plane = lax.dynamic_update_slice(plane, piece[:, None], (0, (y + step) % NY, 0, 0))
    deep = NY * 4 * thin
    plane = after(plane.reshape(3, deep, wide), *near_keys)

    values_in = after(latent[0], got).astype(F32)
    factor = lax.rsqrt(jnp.mean(values_in * values_in, axis=-1, keepdims=True) + 1e-06)
    normed = (values_in * factor * mod_scale[0][None, :] + mod_shift[0][None, :]).astype(BF)
    depth = 2 * deep
    by_z = jnp.transpose(normed.reshape(rows, 4, 4, depth // 4), (2, 0, 1, 3)).reshape(4, rows, depth)
    place = lax.broadcasted_iota(jnp.int32, (depth, depth), 1)
    row = place % thin
    at_xl = place // thin % 2
    at_xh = place // (2 * thin) % 2
    at_y = place // (4 * thin) % 4
    at_c = place // deep
    wanted = (((at_xh * 2 + at_c) * 4 + at_y) * 2 + at_xl) * thin + row
    order = (lax.broadcasted_iota(jnp.int32, (depth, depth), 0) == wanted).astype(BF)
    mine = lax.dot_general(by_z, order, (((2,), (0,)), ((), ())), preferred_element_type=BF)
    theirs = permuted(after(mine, lists, ring), partner)
    kv_got = permuted(after(jnp.stack([keys_sent, values_sent]), theirs), partner)

    where = jnp.stack([z, core]).astype(jnp.int32)
    def along_z_ring(own, steps):
        return own, *(permuted(own, along_z(step)) for step in steps)

    crossed = lambda value: permuted(value, other_core)
    query_weights = along_z_ring(plane[:1], (1, -1, 2))
    fresh_weights = along_z_ring(after(plane[1:], *query_weights[1:]), (1, -1))
    late = after(kv_mine[1:], *query_weights[1:])
    near_values = [permuted(late, along_pairs(step)) for step in (1, -1)]
    across = crossed(plane)
    query_theirs = (across[:1], *map(crossed, query_weights[1:]))

    block = (z * NY + y) * 2 + xl
    other = block + jnp.where(even, 1, -1)
    named = jnp.stack([block, other, block - 2, block + 2, other - 2, other + 2])
    flags = jnp.any(lists[:, None, :] == named[None, :, None], axis=-1).astype(jnp.int32)
    cached = (kv_mine, kv_got, *zip(near_keys, near_values))

    (query,) = project(where, (mine,), query_weights, query_theirs)
    state = attend(flags[0, :4], query, (), cached, (0, 2), ended=False)
    (their_query,) = project(where, (after(theirs, query),), query_weights, query_theirs)
    half = deep // 2
    below, above = after(fresh_weights[1:], query)
    top = permuted(below[:, :half], along_z(1))
    bottom = permuted(above[:, half:], along_z(-1))
    fresh_weights = (*fresh_weights, jnp.concatenate([top, bottom], axis=1))
    late = after(kv_got, top, bottom)
    far = [permuted(late, along_pairs(step)) for step in (1, -1)]
    fresh_theirs = (across[1:], *(crossed(after(w, their_query)) for w in fresh_weights[1:]))
    their_state = attend(flags[1, :4], their_query, (), cached, (0, 2), ended=False)
    their_fresh, fresh = project(where, (after(theirs, *their_state), mine), fresh_weights, fresh_theirs)
    low = attend(flags[1, 4:], their_query, (their_fresh,), far, (0, 1), their_state)
    low_back = permuted(low, partner)
    high = attend(flags[1, 4:], their_query, (their_fresh,), far, (1, 1), their_state)
    high_back = permuted(high, partner)
    own = attend(flags[0, 4:], query, (fresh,), far, (0, 2), state)
    back = jnp.concatenate([low_back, high_back], axis=1)
    return in_order(even, own, back, 1)[None]


def solution(mesh):
    fine = Mesh(mesh.devices.reshape(DIMS), AXES)
    dp, seq = ("xh", "c"), ("z", "y", "xl")
    placed = (
        P(dp, seq, None),
        P(dp, None),
        P(dp, None),
        P(dp + seq, None),
        P(dp + seq, None),
        P(dp + seq, None),
        P(dp, seq, None),
        P(dp, seq, None),
        P(dp, seq, None),
    )
    return jax.shard_map(
        body, mesh=fine, in_specs=placed, out_specs=P(dp, seq, None), check_vma=False
    )
```
